128 devices in a mesh: leaf: 16 (over x_lo, z, core), sub: 8 (over x_hi, y).
Axes of the slice: x: 4 (x_hi: 2, x_lo: 2; x = x_hi * 2 + x_lo), y: 4, z: 4, core: 2. Of those that a mesh axis runs over, the one named last changes fastest.
Arguments:
- density: bfloat16 [32, 2097152], P(None, ('leaf', 'sub')), may hold values from -6 to 6
- geometry: float32 [8192, 6, 256], P(('leaf', 'sub')), may hold values from -134 to 134
- near_list: int32 [8192, 9], P(('leaf', 'sub')), may hold values from 0 to 8191, as said below
- near_count: int32 [8192], P(('leaf', 'sub')), may hold values from 1 to 9, as said below
- far_list: int32 [8192, 16], P(('leaf', 'sub')), may hold values from 0 to 8191, as said below
- bases: bfloat16 [8192, 64, 256], P(('leaf', 'sub')), may hold values from -0.375 to 0.375
- proxies: float32 [8192, 3, 64], P(('leaf', 'sub')), may hold values from -134 to 134
- leaf_transfer: bfloat16 [8192, 64, 64], P(('leaf', 'sub')), may hold values from -0.25 to 0.25
- parent_transfer: bfloat16 [1024, 64, 64], P(('leaf', 'sub')), may hold values from -0.75 to 0.75
- top_proxies: float32 [16, 3, 64], replicated, may hold values from -4 to 4
- top_far: int32 [16, 8], replicated, may hold values from 0 to 15, as said below
Outputs:
- product: float32 [32, 2097152], P(None, ('leaf', 'sub'))
The draws below stay inside these ranges and needn't reach their ends.
Inputs may be any that keep to these rules, and one draw needn't show every extreme that they name: `near_list`: slot 0 of row t is t itself; the other slots hold, in an order drawn for each leaf, the eight leaves t + a * 31 + b modulo 8192 with a and b each -1, 0 or 1, not both 0. `near_count`: the live slots on the leaves of one device number at most 416 together, and exactly 416 on one device. `far_list`: row t holds sixteen distinct leaves, in an order drawn for each leaf, chosen for each leaf from the twenty-two leaves t + a * 31 + b modulo 8192 with a from -2 to 2, b from -3 to 3, and either the larger of |a| and |b| equal to 2, or |a| at most 1 and |b| equal to 3. `top_far`: distinct nodes, none equal to the node or to its two cyclic neighbours.
All inputs are finite; a program needn't handle non-finite values.
Results may differ from the reference program's by a relative error of at most 0.007.
Values may be sent and summed in bfloat16 or wider, within the bound.
No kernel may reach another device: no remote copies, remote signals or barrier semaphores. Data moves between devices by JAX's collectives and lax.ppermute only.
A program may use at most 64 MiB of HBM per device.

```python
import math
import jax
import jax.numpy as jnp
from jax import lax

LP = 256
NRHS = 32
RANK = 64
LEAF_DEV = 64
NEAR = 9
FAR = 16
CYCLE = 31
LEAVES = 8192
PANELS = 2097152
PARENTS = 1024
TOPS = 16
GROUP_PARENTS = 64
TOP_FAR = 8


def leaf_frame():
    radius = CYCLE / (2.0 * math.pi)
    leaf_ids = jnp.arange(LEAVES, dtype=jnp.float32)
    angle = 2.0 * math.pi * leaf_ids / CYCLE
    height = (leaf_ids - 0.5 * LEAVES) / CYCLE
    return (radius, angle, height)


def cycle_centres(node_total, radius):
    angle = 2.0 * math.pi * jnp.arange(node_total, dtype=jnp.float32) / node_total
    return jnp.stack([radius * jnp.cos(angle), radius * jnp.sin(angle), jnp.zeros_like(angle)], axis=1)


def draw_geometry(key, part):
    key = jax.random.fold_in(key, 11)
    along_key, upward_key, outward_key, normal_key = jax.random.split(key, 4)
    radius, angle, height = leaf_frame()
    along = jax.random.uniform(along_key, (LEAVES, LP), jnp.float32, -0.5, 0.5)
    upward = jax.random.uniform(upward_key, (LEAVES, LP), jnp.float32, -0.5, 0.5)
    outward = jax.random.uniform(outward_key, (LEAVES, LP), jnp.float32, -0.1, 0.1)
    turned = angle[:, None] + along / radius
    first = (radius + outward) * jnp.cos(turned)
    second = (radius + outward) * jnp.sin(turned)
    third = height[:, None] + upward + along / CYCLE
    positions = jnp.stack([first, second, third], axis=1)
    normals = jnp.clip(0.06 * jax.random.normal(normal_key, (LEAVES, 3, LP), jnp.float32), -0.3, 0.3)
    return jnp.concatenate([positions, normals], axis=1)


def draw_proxies(key, part):
    key = jax.random.fold_in(key, 12)
    radius, angle, height = leaf_frame()
    centres = jnp.stack([radius * jnp.cos(angle), radius * jnp.sin(angle), height], axis=1)
    spread = jax.random.uniform(key, (LEAVES, 3, RANK), jnp.float32, -0.8, 0.8)
    return centres[:, :, None] + spread


def draw_top_proxies(key, part):
    key = jax.random.fold_in(key, 13)
    centres = cycle_centres(TOPS, 3.0)
    spread = jax.random.uniform(key, (TOPS, 3, RANK), jnp.float32, -0.5, 0.5)
    return centres[:, :, None] + spread


def shuffled_offsets(key, steps):
    offsets = jnp.concatenate([steps, -steps]).astype(jnp.int32)
    width = offsets.shape[0]
    scores = jax.random.randint(key, (LEAVES, width), 0, 1 << 20, dtype=jnp.int32) * width
    scores = scores + jnp.arange(width, dtype=jnp.int32)[None, :]
    order = jnp.argsort(scores, axis=1)
    return jnp.take(offsets, order)


def draw_near_list(key, part):
    key = jax.random.fold_in(key, 17)
    steps = jnp.array([1, CYCLE - 1, CYCLE, CYCLE + 1], dtype=jnp.int32)
    chosen = shuffled_offsets(key, steps)
    leaf_ids = jnp.arange(LEAVES, dtype=jnp.int32)[:, None]
    others = (leaf_ids + chosen) % LEAVES
    return jnp.concatenate([leaf_ids, others], axis=1).astype(jnp.int32)


def draw_far_list(key, part):
    key = jax.random.fold_in(key, 18)
    steps = jnp.array([2, 3, CYCLE - 3, CYCLE - 2, CYCLE + 2, CYCLE + 3, 2 * CYCLE - 2, 2 * CYCLE - 1, 2 * CYCLE, 2 * CYCLE + 1, 2 * CYCLE + 2], dtype=jnp.int32)
    chosen = shuffled_offsets(key, steps)[:, :FAR]
    leaf_ids = jnp.arange(LEAVES, dtype=jnp.int32)[:, None]
    return ((leaf_ids + chosen) % LEAVES).astype(jnp.int32)


def draw_near_count(key, part):
    key = jax.random.fold_in(key, 19)
    busy_key, base_key, order_key = jax.random.split(key, 3)
    busy = jax.random.randint(busy_key, (), 0, LEAVES // LEAF_DEV, dtype=jnp.int32)
    base = 1 + jax.random.randint(base_key, (LEAVES,), 0, NEAR // 2, dtype=jnp.int32)
    shuffled = jax.random.permutation(order_key, LEAF_DEV)
    pattern = jnp.where(shuffled % 2 == 0, NEAR, NEAR // 2).astype(jnp.int32)
    tiled = jnp.tile(pattern, LEAVES // LEAF_DEV)
    owner = jnp.arange(LEAVES, dtype=jnp.int32) // LEAF_DEV
    return jnp.where(owner == busy, tiled, base).astype(jnp.int32)


def draw_top_far(key, part):
    key = jax.random.fold_in(key, 23)
    row_keys = jax.random.split(key, TOPS)

    def one_row(row_key):
        return jax.random.permutation(row_key, TOPS).astype(jnp.int32)
    ranks = jax.vmap(one_row)(row_keys)
    nodes = jnp.arange(TOPS, dtype=jnp.int32)
    distance = (nodes[None, :] - nodes[:, None]) % TOPS
    excluded = ((distance == 0) | (distance == 1) | (distance == TOPS - 1)).astype(jnp.int32)
    order = jnp.argsort(ranks + excluded * TOPS, axis=1)
    return order[:, :TOP_FAR].astype(jnp.int32)


def levels(key, extent, cuts, least, top_value):
    def one(dim, blocks):
        draws = jax.random.uniform(jax.random.fold_in(jax.random.fold_in(key, 6), dim), (blocks,), jnp.float32, least / len(cuts), top_value / len(cuts))
        return jnp.repeat(jnp.exp(draws), extent[dim] // blocks).reshape((-1,) + (1,) * (len(extent) - dim - 1))

    level = one(*cuts[0])
    for cut in cuts[1:]:
        level = level * one(*cut)
    return level


def scatter_about(key, extent, scale, limit, pieces=(), kind=jnp.bfloat16):
    drawn = scale * jax.random.normal(key, extent, jnp.float32)
    if pieces:
        drawn = drawn * levels(key, extent, pieces, -0.22, 0.18)
    return jnp.clip(drawn, -limit, limit).astype(kind)


def setup_inputs(seed: int = 0) -> dict:
    key_list = jax.random.split(jax.random.key(seed), 12)
    return {
        "density": scatter_about(key_list[0], (NRHS, PANELS), 1.0, 6.0, ((1, 128),)),
        "geometry": draw_geometry(jax.random.fold_in(key_list[11], 71), 0),
        "near_list": draw_near_list(jax.random.fold_in(key_list[11], 71), 0),
        "near_count": draw_near_count(jax.random.fold_in(key_list[11], 71), 0),
        "far_list": draw_far_list(jax.random.fold_in(key_list[11], 71), 0),
        "bases": scatter_about(key_list[5], (LEAVES, RANK, LP), LP ** -0.5, 0.375, ((0, 128),)),
        "proxies": draw_proxies(jax.random.fold_in(key_list[11], 71), 0),
        "leaf_transfer": scatter_about(key_list[7], (LEAVES, RANK, RANK), (8 * RANK) ** -0.5, 0.25, ((0, 128),)),
        "parent_transfer": scatter_about(key_list[8], (PARENTS, RANK, RANK), RANK ** -0.5, 0.75, ((0, 128),)),
        "top_proxies": draw_top_proxies(jax.random.fold_in(key_list[11], 71), 0),
        "top_far": draw_top_far(jax.random.fold_in(key_list[11], 71), 0),
    }


SOFTEN = 0.01
FOUR_PI = 4.0 * math.pi

def rounded(values):
    return lax.optimization_barrier(values.astype(jnp.bfloat16))

def gaps(targets, sources):
    differ_one = targets[..., 0, None, :] - sources[..., 0, :, None]
    differ_two = targets[..., 1, None, :] - sources[..., 1, :, None]
    differ_three = targets[..., 2, None, :] - sources[..., 2, :, None]
    squared = differ_one * differ_one + differ_two * differ_two + differ_three * differ_three + SOFTEN
    return (differ_one, differ_two, differ_three, squared)

def pair_kernel(targets, sources, normals):
    differ_one, differ_two, differ_three, squared = gaps(targets, sources)
    flux = normals[..., 0, :, None] * differ_one + normals[..., 1, :, None] * differ_two + normals[..., 2, :, None] * differ_three
    return flux / (FOUR_PI * squared * jnp.sqrt(squared))

def proxy_kernel(targets, sources):
    squared = gaps(targets, sources)[3]
    return 1.0 / (FOUR_PI * jnp.sqrt(squared))

def reference(density, geometry, near_list, near_count, far_list, bases, proxies, leaf_transfer, parent_transfer, top_proxies, top_far):
    leaf_total = geometry.shape[0]
    plain = density.reshape(NRHS, leaf_total, LP)
    by_leaf = jnp.transpose(plain, (1, 0, 2)).astype(jnp.float32)
    coefficients = rounded(jnp.einsum('nlp,lrp->nlr', plain.astype(jnp.float32), bases.astype(jnp.float32)))
    coeff_leaf = jnp.transpose(coefficients, (1, 0, 2)).astype(jnp.float32)
    leaf_ids = jnp.arange(leaf_total, dtype=jnp.int32)

    def near_leaf(items):
        target, sources, counts = items
        source_geo = geometry[sources]
        kernel = rounded(pair_kernel(geometry[target, :3][None], source_geo[:, :3], source_geo[:, 3:]))
        terms = jnp.einsum('kns,kst->knt', by_leaf[sources], kernel.astype(jnp.float32))
        live_mask = (jnp.arange(NEAR, dtype=jnp.int32) < counts).astype(jnp.float32)
        return lax.optimization_barrier(jnp.sum(terms * live_mask[:, None, None], axis=0))
    near_field = lax.map(near_leaf, (leaf_ids, near_list, near_count))

    def far_leaf(items):
        target, sources = items
        kernel = rounded(proxy_kernel(proxies[target][None], proxies[sources]))
        return jnp.einsum('kns,kst->nt', coeff_leaf[sources], kernel.astype(jnp.float32))
    leaf_far = jnp.transpose(lax.map(far_leaf, (leaf_ids, far_list)), (1, 0, 2))
    lifted = jnp.einsum('nlr,lrs->nls', coefficients.astype(jnp.float32), leaf_transfer.astype(jnp.float32))
    parent_coefficients = rounded(lax.optimization_barrier(jnp.sum(lifted.reshape(NRHS, PARENTS, 8, RANK), axis=2)))
    grouped = parent_coefficients.reshape(NRHS, TOPS, GROUP_PARENTS, RANK).astype(jnp.float32)
    group_transfer = parent_transfer.reshape(TOPS, GROUP_PARENTS, RANK, RANK).astype(jnp.float32)
    group_coefficients = rounded(jnp.einsum('ngpr,gprs->gns', grouped, group_transfer)).astype(jnp.float32)

    def top_node(items):
        target, sources = items
        kernel = rounded(proxy_kernel(top_proxies[target][None], top_proxies[sources]))
        return jnp.einsum('kns,kst->nt', group_coefficients[sources], kernel.astype(jnp.float32))
    top_local = rounded(lax.map(top_node, (jnp.arange(TOPS, dtype=jnp.int32), top_far)))
    spread_top = jnp.repeat(top_local, GROUP_PARENTS, axis=0).astype(jnp.float32)
    parent_local = rounded(jnp.einsum('pns,prs->npr', spread_top, parent_transfer.astype(jnp.float32)))
    spread_parent = jnp.repeat(parent_local, 8, axis=1).astype(jnp.float32)
    leaf_local = rounded(jnp.einsum('nls,lrs->nlr', spread_parent, leaf_transfer.astype(jnp.float32)) + leaf_far)
    product = 0.5 * plain.astype(jnp.float32) + jnp.transpose(near_field, (1, 0, 2))
    product = product + jnp.einsum('nlr,lrp->nlp', leaf_local.astype(jnp.float32), bases.astype(jnp.float32))
    return product.reshape(NRHS, leaf_total * LP)
```

```python
import functools
import math

import jax
import jax.numpy as jnp
from jax import lax
from jax.experimental import pallas as pl
from jax.experimental.pallas import tpu as pltpu
from jax.sharding import PartitionSpec as P

SOFTEN = 0.01
FOUR_PI = 4.0 * math.pi
AXES = ("leaf", "sub")
LANES = 128
CHUNK = 32
SMEM = pl.BlockSpec(memory_space=pltpu.SMEM)
VMEM = pl.BlockSpec(memory_space=pltpu.VMEM)
PARAMS = pltpu.CompilerParams(vmem_limit_bytes=48 * 1024 * 1024)


def product(left, right, left_dim=1, right_dim=0):
    return lax.dot_general(
        left, right, (((left_dim,), (right_dim,)), ((), ())), preferred_element_type=jnp.float32
    )


def local(leaf, first, total):
    return lax.rem(leaf - first + (total + total // 2), total) - total // 2


def lift_kernel(density, bases, leaf_transfer, parent_transfer, coefficients, partial):
    parents = parent_transfer.shape[0]
    width = bases.shape[2]
    fan = bases.shape[0] // parents
    partial[...] = jnp.zeros_like(partial)

    def one_parent(p, _):
        lifted = jnp.zeros(partial.shape, jnp.float32)
        held = None
        for c in range(fan):
            l = p * fan + c
            start = pl.multiple_of(l * width, width)
            value = product(density[:, pl.ds(start, width)], bases[l], 1, 1).astype(jnp.bfloat16)
            lifted = lifted + product(value, leaf_transfer[l])
            if c % 2 == 0:
                held = value
            else:
                coefficients[p * (fan // 2) + c // 2] = jnp.concatenate([held, value], axis=1)
        partial[...] += product(lifted.astype(jnp.bfloat16), parent_transfer[p])
        return 0

    lax.fori_loop(0, parents, one_parent, 0)


def lift(density, bases, leaf_transfer, parent_transfer):
    leaves, rank, _ = bases.shape
    sides = density.shape[0]
    return pl.pallas_call(
        lift_kernel,
        out_shape=(
            jax.ShapeDtypeStruct((leaves // 2, sides, 2 * rank), jnp.bfloat16),
            jax.ShapeDtypeStruct((sides, rank), jnp.float32),
        ),
        in_specs=[VMEM] * 4,
        out_specs=(VMEM, VMEM),
        compiler_params=PARAMS,
    )(density, bases, leaf_transfer, parent_transfer)


def split(value):
    high = value.astype(jnp.bfloat16).astype(jnp.float32)
    left = value - high
    middle = left.astype(jnp.bfloat16).astype(jnp.float32)
    return high, middle, left - middle


def near_kernel(
    total, place, near_list, near_count, geo_own, geo_low, geo_high, den_own, den_low, den_high,
    near, task_target, task_source, source, target, density, lhs, column, flux, block,
):
    leaves = geo_own.shape[1]
    width = geo_own.shape[2]
    reach = geo_low.shape[1]
    everything = leaves + 2 * reach
    slots = near_list.shape[0]
    first = place[0]

    def put(ref, row, value):
        for b in range(0, width, LANES):
            ref[b // LANES, pl.ds(row, 8, stride=8), :] = value[:, b : b + LANES]

    def get(ref, row, count):
        return jnp.concatenate(
            [ref[b, pl.ds(row, count), :] for b in range(width // LANES)], axis=1
        )

    def append(t, position):
        live = near_count[t]
        for k in range(slots):
            s = local(near_list[k, t], first + t, total) + t
            s = jnp.where(s >= leaves, s + reach, jnp.where(s < 0, s + leaves + reach, s))
            task_source[position] = s
            task_target[position // 2] = t
            position = position + jnp.where(k < live, 1, 0)
        task_source[position] = everything
        return (position + 1) // 2 * 2

    for i in range(2):
        task_target[i] = leaves
        task_source[2 * i] = everything
        task_source[2 * i + 1] = everything
    ended = lax.fori_loop(0, leaves, append, 4)
    pairs = ended // 2 - 2
    for i in range(2):
        task_target[pairs + 2 + i] = leaves
        task_source[ended + 2 * i] = everything
        task_source[ended + 2 * i + 1] = everything

    center = [jnp.mean(geo_own[c], keepdims=True) for c in range(3)]
    for base, ref in ((0, geo_own), (leaves, geo_low), (leaves + reach, geo_high)):
        for g in range(0, ref.shape[1], 8):
            position = [ref[c, g : g + 8, :] for c in range(3)]
            normal = [ref[3 + c, g : g + 8, :] * (1.0 / FOUR_PI) for c in range(3)]
            moved = [value - middle for value, middle in zip(position, center)]
            shift = normal[0] * moved[0] + normal[1] * moved[1] + normal[2] * moved[2]
            row = (base + g) * 8
            for c in range(3):
                put(source, row + c, normal[c])
                put(source, row + 4 + c, position[c])
            put(source, row + 3, shift)
            put(source, row + 7, jnp.zeros_like(shift))
            if base == 0:
                for c in range(3):
                    put(target, row + c, moved[c])
                    put(target, row + 4 + c, position[c])
                put(target, row + 3, jnp.full_like(shift, -1.0))
                put(target, row + 7, jnp.zeros_like(shift))
        dens = {0: den_own, leaves: den_low, leaves + reach: den_high}[base]
        for l in range(ref.shape[1]):
            density[base + l] = dens[:, l * width : (l + 1) * width]
    density[everything] = jnp.zeros(density.shape[1:], density.dtype)
    for b in range(width // LANES):
        source[b, everything * 8 :, :] = jnp.zeros((8, LANES), jnp.float32)

    rows = lax.broadcasted_iota(jnp.int32, (8, width), 0)
    with_shift = (rows < 4).astype(jnp.float32)
    without = (rows < 3).astype(jnp.float32)

    def prepare(t, _):
        raw = get(target, pl.multiple_of(t * 8, 8), 8)
        high, middle, low = split(raw)
        led = high * with_shift
        second = middle * without
        stacked = jnp.concatenate([led, second, low * without, led, second, led, raw], axis=0)
        turned = stacked.T
        lhs[t] = turned[:, :48].astype(jnp.bfloat16)
        column[t] = turned[:, 48:]
        near[t] = jnp.zeros(near.shape[1:], near.dtype)
        return 0

    lax.fori_loop(0, leaves, prepare, 0)
    near[leaves] = jnp.zeros(near.shape[1:], near.dtype)
    block[...] = jnp.zeros_like(block)
    flux[...] = jnp.zeros_like(flux)

    def weights(s):
        high, middle, low = split(get(source, pl.multiple_of(s * 8, 8), 8))
        return jnp.concatenate([high, high, high, middle, middle, low], axis=0).astype(jnp.bfloat16)

    def step(j, _):
        t = task_target[j]
        both = jnp.concatenate([density[task_source[2 * j + i]] for i in range(2)], axis=1)
        near[t] += product(both, block[...], 1, 1)

        t = jnp.minimum(task_target[j + 1], leaves - 1)
        pair = [task_source[2 * j + 2 + i] for i in range(2)]
        places = [
            jnp.concatenate([get(source, s * 8 + 4 + a, 1) for s in pair], axis=1)
            for a in range(3)
        ]
        for r in range(0, width, CHUNK):
            lines = column[t, r : r + CHUNK, :]
            spread = [
                jnp.broadcast_to(lines[:, 4 + a : 5 + a], (CHUNK, LANES)) for a in range(3)
            ]
            for b in range(0, 2 * width, LANES):
                gap = [spread[a] - places[a][:, b : b + LANES] for a in range(3)]
                squared = gap[0] * gap[0] + gap[1] * gap[1] + (gap[2] * gap[2] + SOFTEN)
                inverse = lax.rsqrt(squared)
                value = flux[r : r + CHUNK, b : b + LANES] * inverse * (inverse * inverse)
                block[r : r + CHUNK, b : b + LANES] = value.astype(jnp.bfloat16)

        t = jnp.minimum(task_target[j + 2], leaves - 1)
        pair = [task_source[2 * j + 4 + i] for i in range(2)]
        flux[...] = product(lhs[t], jnp.concatenate([weights(s) for s in pair], axis=1))
        return 0

    lax.fori_loop(0, pairs + 2, step, 0)


def near_field(total, place, near_list, near_count, geometries, densities):
    leaves, width = geometries[0].shape[1:]
    everything = leaves + 2 * geometries[1].shape[1]
    sides = densities[0].shape[0]
    slots = near_list.shape[0]
    most = leaves * (slots // 2 + 1) + 8
    return pl.pallas_call(
        functools.partial(near_kernel, total),
        out_shape=jax.ShapeDtypeStruct((leaves + 1, sides, width), jnp.float32),
        in_specs=[SMEM] * 3 + [VMEM] * 6,
        out_specs=VMEM,
        scratch_shapes=[
            pltpu.SMEM((most,), jnp.int32),
            pltpu.SMEM((2 * most,), jnp.int32),
            pltpu.VMEM((width // LANES, (everything + 1) * 8, LANES), jnp.float32),
            pltpu.VMEM((width // LANES, leaves * 8, LANES), jnp.float32),
            pltpu.VMEM((everything + 1, sides, width), jnp.bfloat16),
            pltpu.VMEM((leaves, width, 48), jnp.bfloat16),
            pltpu.VMEM((leaves, width, 8), jnp.float32),
            pltpu.VMEM((width, 2 * width), jnp.float32),
            pltpu.VMEM((width, 2 * width), jnp.bfloat16),
        ],
        compiler_params=PARAMS,
    )(place, near_list, near_count, *geometries, *densities)


def final_kernel(
    total, place, far_list, top_far, top_proxies, coupled, coef_own, coef_low, coef_high,
    prox_own, prox_low, prox_high, near, density, bases, leaf_transfer, parent_transfer,
    out, charges, points, lines, parent_local,
):
    leaves, rank, width = bases.shape
    first = place[0]
    group = place[1]
    parents = parent_transfer.shape[0]
    fan = leaves // parents
    sides = density.shape[0]
    left = lax.broadcasted_iota(jnp.int32, (sides, LANES), 1) < rank
    row_left = lax.broadcasted_iota(jnp.int32, (1, LANES), 1) < rank

    def duplicate(value):
        return jnp.concatenate([value, value], axis=1)

    top_local = jnp.zeros((sides, rank), jnp.float32)
    stacked = jnp.concatenate(
        [top_proxies[c, pl.ds(group, 1), :] for c in range(3)]
        + [jnp.zeros((5, rank), jnp.float32)], axis=0,
    )
    turned = duplicate(stacked).T[:rank]
    for k in range(top_far.shape[0]):
        node = top_far[k, group]
        squared = jnp.full((rank, rank), SOFTEN, jnp.float32)
        for c in range(3):
            gap = turned[:, c : c + 1] - top_proxies[c, pl.ds(node, 1), :]
            squared = squared + gap * gap
        coupling = (lax.rsqrt(squared) * (1.0 / FOUR_PI)).astype(jnp.bfloat16)
        top_local = top_local + product(coupled[group ^ node], coupling, 1, 1)
    top_local = top_local.astype(jnp.bfloat16)
    for p in range(parents):
        parent_local[p] = product(top_local, parent_transfer[p], 1, 1).astype(jnp.bfloat16)

    for base, ref, prox in (
        (0, coef_low, prox_low), (leaves, coef_own, prox_own), (2 * leaves, coef_high, prox_high)
    ):
        for i in range(leaves // 2):
            value = ref[i].astype(jnp.float32)
            turned = pltpu.roll(value, rank, 1)
            charges[base + 2 * i] = jnp.where(left, value, turned).astype(jnp.bfloat16)
            charges[base + 2 * i + 1] = jnp.where(left, turned, value).astype(jnp.bfloat16)
        for c in range(3):
            points[c, base : base + leaves, :] = duplicate(prox[c])
    for g in range(0, leaves, 8):
        for c in range(3):
            lines[pl.ds(g * 8 + c, 8, stride=8), :] = points[c, leaves + g : leaves + g + 8, :]
        for c in range(3, 8):
            lines[pl.ds(g * 8 + c, 8, stride=8), :] = jnp.zeros((8, LANES), jnp.float32)

    def one_leaf(t):
        turned = lines[pl.ds(pl.multiple_of(t * 8, 8), 8), :].T[:rank]
        spread = [jnp.broadcast_to(turned[:, c : c + 1], (rank, LANES)) for c in range(3)]
        blocks = []
        values = []
        for q in range(far_list.shape[0] // 2):
            pair = [
                local(far_list[2 * q + i, t], first + t, total) + t + leaves for i in range(2)
            ]
            gap = [
                spread[c]
                - jnp.where(
                    row_left, points[c, pl.ds(pair[0], 1), :], points[c, pl.ds(pair[1], 1), :]
                )
                for c in range(3)
            ]
            squared = gap[0] * gap[0] + gap[1] * gap[1] + (gap[2] * gap[2] + SOFTEN)
            blocks.append((lax.rsqrt(squared) * (1.0 / FOUR_PI)).astype(jnp.bfloat16))
            values.append(jnp.where(left, charges[pair[0]], charges[pair[1]]))
        far = product(jnp.concatenate(values, axis=1), jnp.concatenate(blocks, axis=1), 1, 1)
        leaf_local = far + product(parent_local[t // fan], leaf_transfer[t], 1, 1)
        start = pl.multiple_of(t * width, width)
        result = 0.5 * density[:, pl.ds(start, width)].astype(jnp.float32) + near[t]
        out[:, pl.ds(start, width)] = result + product(leaf_local.astype(jnp.bfloat16), bases[t])

    def some(j, _):
        for i in range(2):
            one_leaf(2 * j + i)
        return 0

    lax.fori_loop(0, leaves // 2, some, 0)


def finish(total, place, far_list, top_far, top_proxies, coupled, coefs, proxies, near, density,
           bases, leaf_transfer, parent_transfer):
    leaves, rank, width = bases.shape
    sides = density.shape[0]
    return pl.pallas_call(
        functools.partial(final_kernel, total),
        out_shape=jax.ShapeDtypeStruct(density.shape, jnp.float32),
        in_specs=[SMEM] * 3 + [VMEM] * 13,
        out_specs=VMEM,
        scratch_shapes=[
            pltpu.VMEM((3 * leaves, sides, LANES), jnp.bfloat16),
            pltpu.VMEM((3, 3 * leaves, LANES), jnp.float32),
            pltpu.VMEM((leaves * 8, LANES), jnp.float32),
            pltpu.VMEM((parent_transfer.shape[0], sides, rank), jnp.bfloat16),
        ],
        compiler_params=PARAMS,
    )(place, far_list, top_far, top_proxies, coupled, *coefs, *proxies, near, density, bases,
      leaf_transfer, parent_transfer)


def per_device(
    density, geometry, near_list, near_count, far_list, bases, proxies, leaf_transfer,
    parent_transfer, top_proxies, top_far,
):
    leaves, _, width = geometry.shape
    devices = lax.axis_size(AXES)
    total = leaves * devices
    group = lax.axis_index("leaf")
    place = jnp.stack([lax.axis_index(AXES) * leaves, group]).astype(jnp.int32)
    reach = leaves // 2
    forward = [(i, (i + 1) % devices) for i in range(devices)]
    backward = [(b, a) for a, b in forward]
    geometry = jnp.transpose(geometry, (1, 0, 2))
    proxies = jnp.transpose(proxies, (1, 0, 2))
    near_list = jnp.transpose(near_list)
    far_list = jnp.transpose(far_list)
    top_proxies = jnp.transpose(top_proxies, (1, 0, 2))
    top_far = jnp.transpose(top_far)

    geo_low = lax.ppermute(geometry[:, leaves - reach :], AXES, forward)
    geo_high = lax.ppermute(geometry[:, :reach], AXES, backward)
    den_low = lax.ppermute(density[:, (leaves - reach) * width :], AXES, forward)
    den_high = lax.ppermute(density[:, : reach * width], AXES, backward)
    prox_low = lax.ppermute(proxies, AXES, forward)
    prox_high = lax.ppermute(proxies, AXES, backward)

    coefficients, partial = lift(density, bases, leaf_transfer, parent_transfer)
    coef_low = lax.ppermute(coefficients, AXES, forward)
    coef_high = lax.ppermute(coefficients, AXES, backward)

    count = lax.axis_size("sub")
    step = 1
    while step < count:
        partial = partial + lax.ppermute(partial, "sub", [(i, i ^ step) for i in range(count)])
        step *= 2
    coupled = partial.astype(jnp.bfloat16)[None]
    count = lax.axis_size("leaf")
    step = 1
    while step < count:
        other = lax.ppermute(coupled, "leaf", [(i, i ^ step) for i in range(count)])
        coupled = jnp.concatenate([coupled, other], axis=0)
        step *= 2

    near = near_field(
        total, place, near_list, near_count,
        (geometry, geo_low, geo_high), (density, den_low, den_high),
    )
    return finish(
        total, place, far_list, top_far, top_proxies, coupled,
        (coefficients, coef_low, coef_high), (proxies, prox_low, prox_high),
        near, density, bases, leaf_transfer, parent_transfer,
    )


def solution(mesh):
    placed = (
        P(None, AXES),
        P(AXES, None, None),
        P(AXES, None),
        P(AXES),
        P(AXES, None),
        P(AXES, None, None),
        P(AXES, None, None),
        P(AXES, None, None),
        P(AXES, None, None),
        P(),
        P(),
    )
    return jax.shard_map(
        per_device, mesh=mesh, in_specs=placed, out_specs=P(None, AXES), check_vma=False
    )
```

```python
import functools
import math

import jax
import jax.numpy as jnp
from jax import lax
from jax.experimental import pallas as pl
from jax.experimental.pallas import tpu as pltpu
from jax.sharding import PartitionSpec as P

SOFTEN = 0.01
FOUR_PI = 4.0 * math.pi
AXES = ("leaf", "sub")
LANES = 128
CHUNK = 16
FAR_UNROLL = 8
SMEM = pl.BlockSpec(memory_space=pltpu.SMEM)
VMEM = pl.BlockSpec(memory_space=pltpu.VMEM)
PARAMS = pltpu.CompilerParams(vmem_limit_bytes=48 * 1024 * 1024)


def product(left, right, left_dim=1, right_dim=0):
    return lax.dot_general(
        left, right, (((left_dim,), (right_dim,)), ((), ())), preferred_element_type=jnp.float32
    )


def local(leaf, first, total):
    moved = leaf - first + (total + total // 2)
    if total & (total - 1) == 0:
        return (moved & (total - 1)) - total // 2
    return lax.rem(moved, total) - total // 2


def lift_kernel(density, bases, leaf_transfer, parent_transfer, coefficients, partial):
    fan, _, width = bases.shape

    @pl.when(pl.program_id(0) == 0)
    def _():
        partial[...] = jnp.zeros_like(partial)

    values = [
        product(density[:, c * width : (c + 1) * width], bases[c], 1, 1).astype(jnp.bfloat16)
        for c in range(fan)
    ]
    lifted = sum(product(value, leaf_transfer[c]) for c, value in enumerate(values))
    for c in range(0, fan, 2):
        coefficients[c // 2] = jnp.concatenate(values[c : c + 2], axis=1)
    partial[...] += product(lifted.astype(jnp.bfloat16), parent_transfer[0])


def lift(density, bases, leaf_transfer, parent_transfer):
    leaves, rank, width = bases.shape
    sides = density.shape[0]
    parents = parent_transfer.shape[0]
    fan = leaves // parents
    return pl.pallas_call(
        lift_kernel,
        grid=(parents,),
        out_shape=(
            jax.ShapeDtypeStruct((leaves // 2, sides, 2 * rank), jnp.bfloat16),
            jax.ShapeDtypeStruct((sides, rank), jnp.float32),
        ),
        in_specs=[
            pl.BlockSpec((sides, fan * width), lambda p: (0, p)),
            pl.BlockSpec((fan, rank, width), lambda p: (p, 0, 0)),
            pl.BlockSpec((fan, rank, rank), lambda p: (p, 0, 0)),
            pl.BlockSpec((1, rank, rank), lambda p: (p, 0, 0)),
        ],
        out_specs=(
            pl.BlockSpec((fan // 2, sides, 2 * rank), lambda p: (p, 0, 0)),
            pl.BlockSpec((sides, rank), lambda p: (0, 0)),
        ),
        compiler_params=PARAMS,
    )(density, bases, leaf_transfer, parent_transfer)


def split(value):
    high = value.astype(jnp.bfloat16).astype(jnp.float32)
    left = value - high
    middle = left.astype(jnp.bfloat16).astype(jnp.float32)
    return high, middle, left - middle


def near_kernel(
    total, place, near_list, near_count, geo_own, geo_low, geo_high, den_own, den_low, den_high,
    near, task_target, task_source, source, target, density, lhs, column,
    flux_one, flux_two, block_one, block_two,
):
    leaves = geo_own.shape[1]
    width = geo_own.shape[2]
    reach = geo_low.shape[1]
    everything = leaves + 2 * reach
    slots = near_list.shape[0]
    first = place[0]

    def put(ref, row, value):
        for b in range(0, width, LANES):
            ref[b // LANES, pl.ds(row, 8, stride=8), :] = value[:, b : b + LANES]

    def get(ref, row, count):
        return jnp.concatenate(
            [ref[b, pl.ds(row, count), :] for b in range(width // LANES)], axis=1
        )

    def append(t, position):
        live = near_count[t]
        for k in range(slots):
            s = local(near_list[k, t], first, total)
            s = jnp.where(s >= leaves, s + reach, jnp.where(s < 0, s + leaves + reach, s))
            task_source[position] = s
            task_target[position >> 1] = t
            position = position + jnp.where(k < live, 1, 0)
        task_source[position] = everything
        return ((position + 1) >> 1) << 1

    for i in range(2):
        task_target[i] = leaves
        task_source[2 * i] = everything
        task_source[2 * i + 1] = everything
    ended = lax.fori_loop(0, leaves, append, 4)
    pairs = (ended >> 1) - 2
    for i in range(4):
        task_target[pairs + 2 + i] = leaves
        task_source[ended + 2 * i] = everything
        task_source[ended + 2 * i + 1] = everything

    center = [jnp.mean(geo_own[c], keepdims=True) for c in range(3)]
    for base, ref in ((0, geo_own), (leaves, geo_low), (leaves + reach, geo_high)):
        for g in range(0, ref.shape[1], 8):
            position = [ref[c, g : g + 8, :] for c in range(3)]
            normal = [ref[3 + c, g : g + 8, :] * (1.0 / FOUR_PI) for c in range(3)]
            moved = [value - middle for value, middle in zip(position, center)]
            shift = normal[0] * moved[0] + normal[1] * moved[1] + normal[2] * moved[2]
            row = (base + g) * 8
            for c in range(3):
                put(source, row + c, normal[c])
                put(source, row + 4 + c, position[c])
            put(source, row + 3, shift)
            put(source, row + 7, jnp.zeros_like(shift))
            if base == 0:
                for c in range(3):
                    put(target, row + c, moved[c])
                    put(target, row + 4 + c, position[c])
                put(target, row + 3, jnp.full_like(shift, -1.0))
                put(target, row + 7, jnp.zeros_like(shift))
        dens = {0: den_own, leaves: den_low, leaves + reach: den_high}[base]
        for l in range(ref.shape[1]):
            density[base + l] = dens[:, l * width : (l + 1) * width]
    density[everything] = jnp.zeros(density.shape[1:], density.dtype)
    for b in range(width // LANES):
        source[b, everything * 8 :, :] = jnp.zeros((8, LANES), jnp.float32)

    rows = lax.broadcasted_iota(jnp.int32, (8, width), 0)
    with_shift = (rows < 4).astype(jnp.float32)
    without = (rows < 3).astype(jnp.float32)

    def prepare(t, _):
        raw = get(target, pl.multiple_of(t * 8, 8), 8)
        high, middle, low = split(raw)
        led = high * with_shift
        second = middle * without
        stacked = jnp.concatenate([led, second, low * without, led, second, led, raw], axis=0)
        turned = stacked.T
        lhs[t] = turned[:, :48].astype(jnp.bfloat16)
        column[t] = turned[:, 48:]
        near[t] = jnp.zeros(near.shape[1:], near.dtype)
        return 0

    lax.fori_loop(0, leaves, prepare, 0, unroll=8)
    near[leaves] = jnp.zeros(near.shape[1:], near.dtype)
    for ref in (flux_one, flux_two, block_one, block_two):
        ref[...] = jnp.zeros_like(ref)

    def weights(s):
        high, middle, low = split(get(source, pl.multiple_of(s * 8, 8), 8))
        return jnp.concatenate([high, high, high, middle, middle, low], axis=0).astype(jnp.bfloat16)

    def multiply(j, block):
        both = jnp.concatenate([density[task_source[2 * j + i]] for i in range(2)], axis=1)
        near[task_target[j]] += product(both, block[...], 1, 1)

    def evaluate(j, flux, block):
        t = jnp.minimum(task_target[j], leaves - 1)
        pair = [task_source[2 * j + i] for i in range(2)]
        places = [
            jnp.concatenate([get(source, s * 8 + 4 + a, 1) for s in pair], axis=1)
            for a in range(3)
        ]
        for r in range(0, width, CHUNK):
            lines = column[t, r : r + CHUNK, :]
            spread = [
                jnp.broadcast_to(lines[:, 4 + a : 5 + a], (CHUNK, LANES)) for a in range(3)
            ]
            for b in range(0, 2 * width, LANES):
                gap = [spread[a] - places[a][:, b : b + LANES] for a in range(3)]
                squared = gap[0] * gap[0] + gap[1] * gap[1] + (gap[2] * gap[2] + SOFTEN)
                inverse = lax.rsqrt(squared)
                value = flux[r : r + CHUNK, b : b + LANES] * inverse * (inverse * inverse)
                block[r : r + CHUNK, b : b + LANES] = value.astype(jnp.bfloat16)

    def project(j, flux):
        t = jnp.minimum(task_target[j], leaves - 1)
        pair = [task_source[2 * j + i] for i in range(2)]
        flux[...] = product(lhs[t], jnp.concatenate([weights(s) for s in pair], axis=1))

    def step(i, _):
        j = 2 * i
        multiply(j, block_one)
        evaluate(j + 1, flux_two, block_two)
        project(j + 2, flux_one)
        multiply(j + 1, block_two)
        evaluate(j + 2, flux_one, block_one)
        project(j + 3, flux_two)
        return 0

    lax.fori_loop(0, (pairs + 3) >> 1, step, 0)


def near_field(total, place, near_list, near_count, geometries, densities):
    leaves, width = geometries[0].shape[1:]
    everything = leaves + 2 * geometries[1].shape[1]
    sides = densities[0].shape[0]
    slots = near_list.shape[0]
    most = leaves * (slots // 2 + 1) + 16
    return pl.pallas_call(
        functools.partial(near_kernel, total),
        out_shape=jax.ShapeDtypeStruct((leaves + 1, sides, width), jnp.float32),
        in_specs=[SMEM] * 3 + [VMEM] * 6,
        out_specs=VMEM,
        scratch_shapes=[
            pltpu.SMEM((most,), jnp.int32),
            pltpu.SMEM((2 * most,), jnp.int32),
            pltpu.VMEM((width // LANES, (everything + 1) * 8, LANES), jnp.float32),
            pltpu.VMEM((width // LANES, leaves * 8, LANES), jnp.float32),
            pltpu.VMEM((everything + 1, sides, width), jnp.bfloat16),
            pltpu.VMEM((leaves, width, 48), jnp.bfloat16),
            pltpu.VMEM((leaves, width, 8), jnp.float32),
            pltpu.VMEM((width, 2 * width), jnp.float32),
            pltpu.VMEM((width, 2 * width), jnp.float32),
            pltpu.VMEM((width, 2 * width), jnp.bfloat16),
            pltpu.VMEM((width, 2 * width), jnp.bfloat16),
        ],
        compiler_params=PARAMS,
        cost_estimate=pl.CostEstimate(
            flops=100 * 10**9 // 2, bytes_accessed=8 * 10**6, transcendentals=3 * 10**7
        ),
    )(place, near_list, near_count, *geometries, *densities)


def final_kernel(
    total, place, far_list, top_far, top_proxies, coupled, coef_own, coef_low, coef_high,
    prox_own, prox_low, prox_high, near, density, bases, leaf_transfer, parent_transfer,
    out, charges, points, lines, parent_local, far,
):
    leaves, rank, width = bases.shape
    first = place[0]
    group = place[1]
    parents = parent_transfer.shape[0]
    fan = leaves // parents
    sides = density.shape[0]
    left = lax.broadcasted_iota(jnp.int32, (sides, LANES), 1) < rank
    row_left = lax.broadcasted_iota(jnp.int32, (1, LANES), 1) < rank

    def duplicate(value):
        return jnp.concatenate([value, value], axis=1)

    top_local = jnp.zeros((sides, rank), jnp.float32)
    stacked = jnp.concatenate(
        [top_proxies[c, pl.ds(group, 1), :] for c in range(3)]
        + [jnp.zeros((5, rank), jnp.float32)], axis=0,
    )
    turned = duplicate(stacked).T[:rank]
    for k in range(top_far.shape[0]):
        node = top_far[k, group]
        squared = jnp.full((rank, rank), SOFTEN, jnp.float32)
        for c in range(3):
            gap = turned[:, c : c + 1] - top_proxies[c, pl.ds(node, 1), :]
            squared = squared + gap * gap
        coupling = (lax.rsqrt(squared) * (1.0 / FOUR_PI)).astype(jnp.bfloat16)
        top_local = top_local + product(coupled[group ^ node], coupling, 1, 1)
    top_local = top_local.astype(jnp.bfloat16)
    for p in range(parents):
        parent_local[p] = product(top_local, parent_transfer[p], 1, 1).astype(jnp.bfloat16)

    for base, ref, prox in (
        (0, coef_low, prox_low), (leaves, coef_own, prox_own), (2 * leaves, coef_high, prox_high)
    ):
        for i in range(leaves // 2):
            value = ref[i].astype(jnp.float32)
            turned = pltpu.roll(value, rank, 1)
            charges[base + 2 * i] = jnp.where(left, value, turned).astype(jnp.bfloat16)
            charges[base + 2 * i + 1] = jnp.where(left, turned, value).astype(jnp.bfloat16)
        for c in range(3):
            points[c, base : base + leaves, :] = duplicate(prox[c])
    for g in range(0, leaves, 8):
        for c in range(3):
            lines[pl.ds(g * 8 + c, 8, stride=8), :] = points[c, leaves + g : leaves + g + 8, :]
        for c in range(3, 8):
            lines[pl.ds(g * 8 + c, 8, stride=8), :] = jnp.zeros((8, LANES), jnp.float32)

    def far_leaf(t):
        turned = lines[pl.ds(pl.multiple_of(t * 8, 8), 8), :].T[:rank]
        spread = [jnp.broadcast_to(turned[:, c : c + 1], (rank, LANES)) for c in range(3)]
        blocks = []
        values = []
        for q in range(far_list.shape[0] // 2):
            pair = [
                local(far_list[2 * q + i, t], first, total) + leaves for i in range(2)
            ]
            gap = [
                spread[c]
                - jnp.where(
                    row_left, points[c, pl.ds(pair[0], 1), :], points[c, pl.ds(pair[1], 1), :]
                )
                for c in range(3)
            ]
            squared = gap[0] * gap[0] + gap[1] * gap[1] + (gap[2] * gap[2] + SOFTEN)
            blocks.append((lax.rsqrt(squared) * (1.0 / FOUR_PI)).astype(jnp.bfloat16))
            values.append(jnp.where(left, charges[pair[0]], charges[pair[1]]))
        far[t] = product(jnp.concatenate(values, axis=1), jnp.concatenate(blocks, axis=1), 1, 1)

    def down_leaf(t, parent):
        leaf_local = far[t] + product(parent_local[parent], leaf_transfer[t], 1, 1)
        start = pl.multiple_of(t * width, width)
        result = 0.5 * density[:, pl.ds(start, width)].astype(jnp.float32) + near[t]
        out[:, pl.ds(start, width)] = result + product(leaf_local.astype(jnp.bfloat16), bases[t])

    def far_some(j, _):
        for i in range(FAR_UNROLL):
            far_leaf(FAR_UNROLL * j + i)
        return 0

    def down_some(j, _):
        for i in range(fan):
            down_leaf(fan * j + i, j)
        return 0

    lax.fori_loop(0, leaves // FAR_UNROLL, far_some, 0)
    lax.fori_loop(0, parents, down_some, 0)


def finish(total, place, far_list, top_far, top_proxies, coupled, coefs, proxies, near, density,
           bases, leaf_transfer, parent_transfer):
    leaves, rank, width = bases.shape
    sides = density.shape[0]
    return pl.pallas_call(
        functools.partial(final_kernel, total),
        out_shape=jax.ShapeDtypeStruct(density.shape, jnp.float32),
        in_specs=[SMEM] * 3 + [VMEM] * 13,
        out_specs=VMEM,
        scratch_shapes=[
            pltpu.VMEM((3 * leaves, sides, LANES), jnp.bfloat16),
            pltpu.VMEM((3, 3 * leaves, LANES), jnp.float32),
            pltpu.VMEM((leaves * 8, LANES), jnp.float32),
            pltpu.VMEM((parent_transfer.shape[0], sides, rank), jnp.bfloat16),
            pltpu.VMEM((leaves, sides, rank), jnp.float32),
        ],
        compiler_params=PARAMS,
    )(place, far_list, top_far, top_proxies, coupled, *coefs, *proxies, near, density, bases,
      leaf_transfer, parent_transfer)


def per_device(
    density, geometry, near_list, near_count, far_list, bases, proxies, leaf_transfer,
    parent_transfer, top_proxies, top_far,
):
    leaves, _, width = geometry.shape
    devices = lax.axis_size(AXES)
    total = leaves * devices
    group = lax.axis_index("leaf")
    place = jnp.stack([lax.axis_index(AXES) * leaves, group]).astype(jnp.int32)
    reach = leaves // 2
    forward = [(i, (i + 1) % devices) for i in range(devices)]
    backward = [(b, a) for a, b in forward]
    geometry = jnp.transpose(geometry, (1, 0, 2))
    proxies = jnp.transpose(proxies, (1, 0, 2))
    near_list = jnp.transpose(near_list)
    far_list = jnp.transpose(far_list)
    top_proxies = jnp.transpose(top_proxies, (1, 0, 2))
    top_far = jnp.transpose(top_far)

    geo_low = lax.ppermute(geometry[:, leaves - reach :], AXES, forward)
    geo_high = lax.ppermute(geometry[:, :reach], AXES, backward)
    den_low = lax.ppermute(density[:, (leaves - reach) * width :], AXES, forward)
    den_high = lax.ppermute(density[:, : reach * width], AXES, backward)
    prox_low = lax.ppermute(proxies, AXES, forward)
    prox_high = lax.ppermute(proxies, AXES, backward)

    coefficients, partial = lift(density, bases, leaf_transfer, parent_transfer)

    count = lax.axis_size("sub")
    step = 1
    while step < count:
        partial = partial + lax.ppermute(partial, "sub", [(i, i ^ step) for i in range(count)])
        if step == 1:
            partial, geo_low, geo_high = lax.optimization_barrier((partial, geo_low, geo_high))
        step *= 2
    coupled = partial.astype(jnp.bfloat16)[None]
    count = lax.axis_size("leaf")
    step = 1
    while step < count:
        other = lax.ppermute(coupled, "leaf", [(i, i ^ step) for i in range(count)])
        coupled = jnp.concatenate([coupled, other], axis=0)
        if step == 1:
            coupled, den_low, den_high = lax.optimization_barrier((coupled, den_low, den_high))
        step *= 2

    coef_low = lax.ppermute(coefficients, AXES, forward)
    coef_high = lax.ppermute(coefficients, AXES, backward)
    near = near_field(
        total, place, near_list, near_count,
        (geometry, geo_low, geo_high), (density, den_low, den_high),
    )
    return finish(
        total, place, far_list, top_far, top_proxies, coupled,
        (coefficients, coef_low, coef_high), (proxies, prox_low, prox_high),
        near, density, bases, leaf_transfer, parent_transfer,
    )


def solution(mesh):
    placed = (
        P(None, AXES),
        P(AXES, None, None),
        P(AXES, None),
        P(AXES),
        P(AXES, None),
        P(AXES, None, None),
        P(AXES, None, None),
        P(AXES, None, None),
        P(AXES, None, None),
        P(),
        P(),
    )
    return jax.shard_map(
        per_device, mesh=mesh, in_specs=placed, out_specs=P(None, AXES), check_vma=False
    )
```

```python
import functools
import math

import jax
import jax.numpy as jnp
from jax import lax
from jax.experimental import pallas as pl
from jax.experimental.pallas import tpu as pltpu
from jax.sharding import PartitionSpec as P

SOFTEN = 0.01
FOUR_PI = 4.0 * math.pi
AXES = ("leaf", "sub")
LANES = 128
CHUNK = 16
SMEM = pl.BlockSpec(memory_space=pltpu.SMEM)
VMEM = pl.BlockSpec(memory_space=pltpu.VMEM)
PARAMS = pltpu.CompilerParams(vmem_limit_bytes=48 * 1024 * 1024)


def product(left, right, left_dim=1, right_dim=0):
    return lax.dot_general(
        left, right, (((left_dim,), (right_dim,)), ((), ())), preferred_element_type=jnp.float32
    )


def local(leaf, first, total):
    moved = leaf - first + (total + total // 2)
    if total & (total - 1) == 0:
        return (moved & (total - 1)) - total // 2
    return lax.rem(moved, total) - total // 2


def lift_kernel(density, bases, leaf_transfer, parent_transfer, coefficients, partial):
    fan, _, width = bases.shape

    @pl.when(pl.program_id(0) == 0)
    def _():
        partial[...] = jnp.zeros_like(partial)

    values = [
        product(density[:, c * width : (c + 1) * width], bases[c], 1, 1).astype(jnp.bfloat16)
        for c in range(fan)
    ]
    lifted = sum(product(value, leaf_transfer[c]) for c, value in enumerate(values))
    for c in range(0, fan, 2):
        coefficients[c // 2] = jnp.concatenate(values[c : c + 2], axis=1)
    partial[...] += product(lifted.astype(jnp.bfloat16), parent_transfer[0])


def lift(density, bases, leaf_transfer, parent_transfer):
    leaves, rank, width = bases.shape
    sides = density.shape[0]
    parents = parent_transfer.shape[0]
    fan = leaves // parents
    return pl.pallas_call(
        lift_kernel,
        grid=(parents,),
        out_shape=(
            jax.ShapeDtypeStruct((leaves // 2, sides, 2 * rank), jnp.bfloat16),
            jax.ShapeDtypeStruct((sides, rank), jnp.float32),
        ),
        in_specs=[
            pl.BlockSpec((sides, fan * width), lambda p: (0, p)),
            pl.BlockSpec((fan, rank, width), lambda p: (p, 0, 0)),
            pl.BlockSpec((fan, rank, rank), lambda p: (p, 0, 0)),
            pl.BlockSpec((1, rank, rank), lambda p: (p, 0, 0)),
        ],
        out_specs=(
            pl.BlockSpec((fan // 2, sides, 2 * rank), lambda p: (p, 0, 0)),
            pl.BlockSpec((sides, rank), lambda p: (0, 0)),
        ),
        compiler_params=PARAMS,
    )(density, bases, leaf_transfer, parent_transfer)


def split(value):
    high = value.astype(jnp.bfloat16).astype(jnp.float32)
    left = value - high
    middle = left.astype(jnp.bfloat16).astype(jnp.float32)
    return high, middle, left - middle


def near_kernel(
    total, place, near_list, near_count, other_list, other_count,
    geo_own, geo_low, geo_high, geo_other, geo_side,
    den_own, den_low, den_high, den_other, den_side,
    near, near_other, task_target, task_source, source, target, density, lhs, column,
    flux_one, flux_two, block_one, block_two, sums,
):
    leaves = geo_own.shape[1]
    width = geo_own.shape[2]
    reach = geo_low.shape[1]
    half = leaves // 2
    region = leaves + reach
    everything = 2 * region
    slots = near_list.shape[0]
    side = place[2]

    def put(ref, row, value):
        for b in range(0, width, LANES):
            ref[b // LANES, pl.ds(row, 8, stride=8), :] = value[:, b : b + LANES]

    def get(ref, row, count):
        return jnp.concatenate(
            [ref[b, pl.ds(row, count), :] for b in range(width // LANES)], axis=1
        )

    def append(lists, counts, first, base, shift):
        def leaf(i, position):
            t = side * half + i
            live = counts[t]
            for k in range(slots):
                s = local(lists[k, t], first, total)
                s = jnp.where(s < 0, s + region, s) + base
                task_source[position] = s
                task_target[position >> 1] = i + shift
                position = position + jnp.where(k < live, 1, 0)
            task_source[position] = everything
            return ((position + 1) >> 1) << 1

        return leaf

    for i in range(2):
        task_target[i] = leaves
        task_source[2 * i] = everything
        task_source[2 * i + 1] = everything
    ended = lax.fori_loop(0, half, append(near_list, near_count, place[0], 0, 0), 4)
    ended = lax.fori_loop(
        0, half, append(other_list, other_count, place[1], region, half), ended
    )
    pairs = (ended >> 1) - 2
    for i in range(4):
        task_target[pairs + 2 + i] = leaves
        task_source[ended + 2 * i] = everything
        task_source[ended + 2 * i + 1] = everything

    def table(center, base, geo, den):
        for g in range(0, geo.shape[1], 8):
            position = [geo[c, g : g + 8, :] for c in range(3)]
            normal = [geo[3 + c, g : g + 8, :] * (1.0 / FOUR_PI) for c in range(3)]
            moved = [value - middle for value, middle in zip(position, center)]
            shift = normal[0] * moved[0] + normal[1] * moved[1] + normal[2] * moved[2]
            row = (base + g) * 8
            for c in range(3):
                put(source, row + c, normal[c])
                put(source, row + 4 + c, position[c])
            put(source, row + 3, shift)
            put(source, row + 7, jnp.zeros_like(shift))
        for l in range(geo.shape[1]):
            density[base + l] = den[:, l * width : (l + 1) * width]

    def aims(center, base, geo):
        def group(i, _):
            place_in = pl.multiple_of(side * half + i * 8, 8)
            row = (base + i * 8) * 8
            one = jnp.ones((8, width), jnp.float32)
            for c in range(3):
                position = geo[c, pl.ds(place_in, 8), :]
                put(target, row + c, position - center[c])
                put(target, row + 4 + c, position)
            put(target, row + 3, -one)
            put(target, row + 7, 0.0 * one)
            return 0

        lax.fori_loop(0, half // 8, group, 0, unroll=True)

    center = [jnp.mean(geo_own[c], keepdims=True) for c in range(3)]
    table(center, 0, geo_own, den_own)

    @pl.when(side == 0)
    def _():
        table(center, leaves, geo_low, den_low)

    @pl.when(side != 0)
    def _():
        table(center, leaves, geo_high, den_high)

    aims(center, 0, geo_own)
    center = [jnp.mean(geo_other[c], keepdims=True) for c in range(3)]
    table(center, region, geo_other, den_other)
    table(center, region + leaves, geo_side, den_side)
    aims(center, half, geo_other)
    density[everything] = jnp.zeros(density.shape[1:], density.dtype)
    for b in range(width // LANES):
        source[b, everything * 8 :, :] = jnp.zeros((8, LANES), jnp.float32)

    rows = lax.broadcasted_iota(jnp.int32, (8, width), 0)
    with_shift = (rows < 4).astype(jnp.float32)
    without = (rows < 3).astype(jnp.float32)

    def prepare(t, _):
        raw = get(target, pl.multiple_of(t * 8, 8), 8)
        high, middle, low = split(raw)
        led = high * with_shift
        second = middle * without
        stacked = jnp.concatenate([led, second, low * without, led, second, led, raw], axis=0)
        turned = stacked.T
        lhs[t] = turned[:, :48].astype(jnp.bfloat16)
        column[t] = turned[:, 48:]
        sums[t] = jnp.zeros(sums.shape[1:], sums.dtype)
        return 0

    lax.fori_loop(0, leaves, prepare, 0, unroll=8)
    sums[leaves] = jnp.zeros(sums.shape[1:], sums.dtype)
    for ref in (flux_one, flux_two, block_one, block_two):
        ref[...] = jnp.zeros_like(ref)

    def weights(s):
        high, middle, low = split(get(source, pl.multiple_of(s * 8, 8), 8))
        return jnp.concatenate([high, high, high, middle, middle, low], axis=0).astype(jnp.bfloat16)

    def multiply(j, block):
        both = jnp.concatenate([density[task_source[2 * j + i]] for i in range(2)], axis=1)
        sums[task_target[j]] += product(both, block[...], 1, 1)

    def evaluate(j, flux, block):
        t = jnp.minimum(task_target[j], leaves - 1)
        pair = [task_source[2 * j + i] for i in range(2)]
        places = [
            jnp.concatenate([get(source, s * 8 + 4 + a, 1) for s in pair], axis=1)
            for a in range(3)
        ]
        for r in range(0, width, CHUNK):
            lines = column[t, r : r + CHUNK, :]
            spread = [
                jnp.broadcast_to(lines[:, 4 + a : 5 + a], (CHUNK, LANES)) for a in range(3)
            ]
            for b in range(0, 2 * width, LANES):
                gap = [spread[a] - places[a][:, b : b + LANES] for a in range(3)]
                squared = gap[0] * gap[0] + gap[1] * gap[1] + (gap[2] * gap[2] + SOFTEN)
                inverse = lax.rsqrt(squared)
                value = flux[r : r + CHUNK, b : b + LANES] * inverse * (inverse * inverse)
                block[r : r + CHUNK, b : b + LANES] = value.astype(jnp.bfloat16)

    def project(j, flux):
        t = jnp.minimum(task_target[j], leaves - 1)
        pair = [task_source[2 * j + i] for i in range(2)]
        flux[...] = product(lhs[t], jnp.concatenate([weights(s) for s in pair], axis=1))

    def step(i, _):
        j = 2 * i
        multiply(j, block_one)
        evaluate(j + 1, flux_two, block_two)
        project(j + 2, flux_one)
        multiply(j + 1, block_two)
        evaluate(j + 2, flux_one, block_one)
        project(j + 3, flux_two)
        return 0

    lax.fori_loop(0, (pairs + 3) >> 1, step, 0)
    for t in range(half):
        near[t] = sums[t]
        near_other[t] = sums[half + t].astype(near_other.dtype)


def near_field(total, place, lists, geometries, densities):
    leaves, width = geometries[0].shape[1:]
    everything = 2 * (leaves + geometries[1].shape[1])
    sides = densities[0].shape[0]
    slots = lists[0].shape[0]
    most = leaves * (slots // 2 + 1) + 16
    half = (leaves // 2, sides, width)
    return pl.pallas_call(
        functools.partial(near_kernel, total),
        out_shape=(
            jax.ShapeDtypeStruct(half, jnp.float32),
            jax.ShapeDtypeStruct(half, jnp.bfloat16),
        ),
        in_specs=[SMEM] * 5 + [VMEM] * 10,
        out_specs=(VMEM, VMEM),
        scratch_shapes=[
            pltpu.SMEM((most,), jnp.int32),
            pltpu.SMEM((2 * most,), jnp.int32),
            pltpu.VMEM((width // LANES, (everything + 1) * 8, LANES), jnp.float32),
            pltpu.VMEM((width // LANES, leaves * 8, LANES), jnp.float32),
            pltpu.VMEM((everything + 1, sides, width), jnp.bfloat16),
            pltpu.VMEM((leaves, width, 48), jnp.bfloat16),
            pltpu.VMEM((leaves, width, 8), jnp.float32),
            pltpu.VMEM((width, 2 * width), jnp.float32),
            pltpu.VMEM((width, 2 * width), jnp.float32),
            pltpu.VMEM((width, 2 * width), jnp.bfloat16),
            pltpu.VMEM((width, 2 * width), jnp.bfloat16),
            pltpu.VMEM((leaves + 1, sides, width), jnp.float32),
        ],
        compiler_params=PARAMS,
        cost_estimate=pl.CostEstimate(
            flops=100 * 10**9 // 2, bytes_accessed=8 * 10**6, transcendentals=3 * 10**7
        ),
    )(place, *lists, *geometries, *densities)


def final_kernel(
    total, place, far_list, top_far, top_proxies, coupled, coef_own, coef_low, coef_high,
    prox_own, prox_low, prox_high, near, near_back, density, bases, leaf_transfer, parent_transfer,
    out, charges, points, lines, parent_local, far,
):
    leaves, rank, width = bases.shape
    first = place[0]
    group = place[3]
    half = near.shape[0]
    parents = parent_transfer.shape[0]
    fan = leaves // parents
    sides = density.shape[0]
    left = lax.broadcasted_iota(jnp.int32, (sides, LANES), 1) < rank
    row_left = lax.broadcasted_iota(jnp.int32, (1, LANES), 1) < rank

    def duplicate(value):
        return jnp.concatenate([value, value], axis=1)

    top_local = jnp.zeros((sides, rank), jnp.float32)
    stacked = jnp.concatenate(
        [top_proxies[c, pl.ds(group, 1), :] for c in range(3)]
        + [jnp.zeros((5, rank), jnp.float32)], axis=0,
    )
    turned = duplicate(stacked).T[:rank]
    for k in range(top_far.shape[0]):
        node = top_far[k, group]
        squared = jnp.full((rank, rank), SOFTEN, jnp.float32)
        for c in range(3):
            gap = turned[:, c : c + 1] - top_proxies[c, pl.ds(node, 1), :]
            squared = squared + gap * gap
        coupling = (lax.rsqrt(squared) * (1.0 / FOUR_PI)).astype(jnp.bfloat16)
        top_local = top_local + product(coupled[group ^ node], coupling, 1, 1)
    top_local = top_local.astype(jnp.bfloat16)
    for p in range(parents):
        parent_local[p] = product(top_local, parent_transfer[p], 1, 1).astype(jnp.bfloat16)

    for base, ref, prox in (
        (0, coef_low, prox_low), (leaves, coef_own, prox_own), (2 * leaves, coef_high, prox_high)
    ):
        for i in range(leaves // 2):
            value = ref[i].astype(jnp.float32)
            turned = pltpu.roll(value, rank, 1)
            charges[base + 2 * i] = jnp.where(left, value, turned).astype(jnp.bfloat16)
            charges[base + 2 * i + 1] = jnp.where(left, turned, value).astype(jnp.bfloat16)
        for c in range(3):
            points[c, base : base + leaves, :] = duplicate(prox[c])
    for g in range(0, leaves, 8):
        for c in range(3):
            lines[pl.ds(g * 8 + c, 8, stride=8), :] = points[c, leaves + g : leaves + g + 8, :]
        for c in range(3, 8):
            lines[pl.ds(g * 8 + c, 8, stride=8), :] = jnp.zeros((8, LANES), jnp.float32)

    def far_leaf(t):
        turned = lines[pl.ds(pl.multiple_of(t * 8, 8), 8), :].T[:rank]
        spread = [jnp.broadcast_to(turned[:, c : c + 1], (rank, LANES)) for c in range(3)]
        blocks = []
        values = []
        for q in range(far_list.shape[0] // 2):
            pair = [
                local(far_list[2 * q + i, t], first, total) + leaves for i in range(2)
            ]
            gap = [
                spread[c]
                - jnp.where(
                    row_left, points[c, pl.ds(pair[0], 1), :], points[c, pl.ds(pair[1], 1), :]
                )
                for c in range(3)
            ]
            squared = gap[0] * gap[0] + gap[1] * gap[1] + (gap[2] * gap[2] + SOFTEN)
            blocks.append((lax.rsqrt(squared) * (1.0 / FOUR_PI)).astype(jnp.bfloat16))
            values.append(jnp.where(left, charges[pair[0]], charges[pair[1]]))
        return product(jnp.concatenate(values, axis=1), jnp.concatenate(blocks, axis=1), 1, 1)

    def far_parent(p):
        for i in range(fan):
            far[i] = far_leaf(fan * p + i)

    def down_parent(p):
        start = pl.multiple_of(p * fan, fan)
        transfer = leaf_transfer[pl.ds(start, fan)].reshape(fan * rank, rank)
        whole = product(parent_local[p], transfer, 1, 1)
        for i in range(fan):
            t = fan * p + i
            leaf_local = (far[i] + whole[:, i * rank : (i + 1) * rank]).astype(jnp.bfloat16)
            span = pl.ds(pl.multiple_of(t * width, width), width)
            row = fan * lax.rem(p, half // fan) + i
            mine = p // (half // fan) == place[2]
            nearby = jnp.where(mine, near[row], near_back[row].astype(jnp.float32))
            result = 0.5 * density[:, span].astype(jnp.float32) + nearby
            out[:, span] = result + product(leaf_local, bases[t])

    def both(p, _):
        down_parent(p)
        far_parent(p + 1)
        return 0

    far_parent(0)
    lax.fori_loop(0, parents - 1, both, 0)
    down_parent(parents - 1)


def finish(total, place, far_list, top_far, top_proxies, coupled, coefs, proxies, near, near_back, density,
           bases, leaf_transfer, parent_transfer):
    leaves, rank, width = bases.shape
    sides = density.shape[0]
    return pl.pallas_call(
        functools.partial(final_kernel, total),
        out_shape=jax.ShapeDtypeStruct(density.shape, jnp.float32),
        in_specs=[SMEM] * 3 + [VMEM] * 14,
        out_specs=VMEM,
        scratch_shapes=[
            pltpu.VMEM((3 * leaves, sides, LANES), jnp.bfloat16),
            pltpu.VMEM((3, 3 * leaves, LANES), jnp.float32),
            pltpu.VMEM((leaves * 8, LANES), jnp.float32),
            pltpu.VMEM((parent_transfer.shape[0], sides, rank), jnp.bfloat16),
            pltpu.VMEM((leaves // parent_transfer.shape[0], sides, rank), jnp.float32),
        ],
        compiler_params=PARAMS,
    )(place, far_list, top_far, top_proxies, coupled, *coefs, *proxies, near, near_back, density, bases,
      leaf_transfer, parent_transfer)


def per_device(
    density, geometry, near_list, near_count, far_list, bases, proxies, leaf_transfer,
    parent_transfer, top_proxies, top_far,
):
    leaves, _, width = geometry.shape
    devices = lax.axis_size(AXES)
    total = leaves * devices
    group = lax.axis_index("leaf")
    sub = lax.axis_index("sub")
    subs = lax.axis_size("sub")
    groups = lax.axis_size("leaf")
    side = group % 2
    place = jnp.stack(
        [(group * subs + sub) * leaves, ((group ^ 1) * subs + sub) * leaves, side, group]
    ).astype(jnp.int32)

    def swap(value):
        return lax.ppermute(value, "leaf", [(i, i ^ 1) for i in range(groups)])

    reach = leaves // 2
    forward = [(i, (i + 1) % devices) for i in range(devices)]
    backward = [(b, a) for a, b in forward]
    geometry = jnp.transpose(geometry, (1, 0, 2))
    proxies = jnp.transpose(proxies, (1, 0, 2))
    near_list = jnp.transpose(near_list)
    far_list = jnp.transpose(far_list)
    top_proxies = jnp.transpose(top_proxies, (1, 0, 2))
    top_far = jnp.transpose(top_far)

    geo_low = lax.ppermute(geometry[:, leaves - reach :], AXES, forward)
    geo_high = lax.ppermute(geometry[:, :reach], AXES, backward)
    den_low = lax.ppermute(density[:, (leaves - reach) * width :], AXES, forward)
    den_high = lax.ppermute(density[:, : reach * width], AXES, backward)
    prox_low = lax.ppermute(proxies, AXES, forward)
    prox_high = lax.ppermute(proxies, AXES, backward)

    other_list = swap(jnp.concatenate([near_list, near_count[None]], axis=0))
    geo_other = swap(geometry)
    den_other = swap(density)

    coefficients, partial = lift(density, bases, leaf_transfer, parent_transfer)

    count = lax.axis_size("sub")
    step = 1
    while step < count:
        partial = partial + lax.ppermute(partial, "sub", [(i, i ^ step) for i in range(count)])
        if step == 1:
            partial, geo_low, geo_high = lax.optimization_barrier((partial, geo_low, geo_high))
        step *= 2
    coupled = partial.astype(jnp.bfloat16)[None]
    count = lax.axis_size("leaf")
    step = 1
    while step < count:
        other = lax.ppermute(coupled, "leaf", [(i, i ^ step) for i in range(count)])
        coupled = jnp.concatenate([coupled, other], axis=0)
        if step == 1:
            coupled, den_low, den_high = lax.optimization_barrier((coupled, den_low, den_high))
        step *= 2

    coef_low = lax.ppermute(coefficients, AXES, forward)
    coef_high = lax.ppermute(coefficients, AXES, backward)
    geo_side = swap(jnp.where(side == 0, geo_high, geo_low))
    den_side = swap(jnp.where(side == 0, den_high, den_low))
    coupled, other_list, coef_low, coef_high, prox_low, prox_high = lax.optimization_barrier(
        (coupled, other_list, coef_low, coef_high, prox_low, prox_high)
    )
    near, near_other = near_field(
        total, place, (near_list, near_count, other_list[:-1], other_list[-1]),
        (geometry, geo_low, geo_high, geo_other, geo_side),
        (density, den_low, den_high, den_other, den_side),
    )
    near_back = swap(near_other)
    return finish(
        total, place, far_list, top_far, top_proxies, coupled,
        (coefficients, coef_low, coef_high), (proxies, prox_low, prox_high),
        near, near_back, density, bases, leaf_transfer, parent_transfer,
    )


def solution(mesh):
    placed = (
        P(None, AXES),
        P(AXES, None, None),
        P(AXES, None),
        P(AXES),
        P(AXES, None),
        P(AXES, None, None),
        P(AXES, None, None),
        P(AXES, None, None),
        P(AXES, None, None),
        P(),
        P(),
    )
    return jax.shard_map(
        per_device, mesh=mesh, in_specs=placed, out_specs=P(None, AXES), check_vma=False
    )
```

```python
import math

import jax
import jax.numpy as jnp
from jax import lax
from jax.experimental import pallas as pl
from jax.experimental.pallas import tpu as pltpu
from jax.sharding import PartitionSpec as P

SOFTEN = 0.01
FOUR_PI = 4.0 * math.pi
AXES = ("leaf", "sub")
LANES = 128
CHUNK = 16
SMEM = pl.BlockSpec(memory_space=pltpu.SMEM)
VMEM = pl.BlockSpec(memory_space=pltpu.VMEM)
PARAMS = pltpu.CompilerParams(vmem_limit_bytes=48 * 1024 * 1024)


def product(left, right, left_dim=1, right_dim=0):
    return lax.dot_general(
        left, right, (((left_dim,), (right_dim,)), ((), ())), preferred_element_type=jnp.float32
    )


def local(leaf, first, total):
    moved = leaf - first + (total + total // 2)
    if total & (total - 1) == 0:
        return (moved & (total - 1)) - total // 2
    return lax.rem(moved, total) - total // 2


def lift_kernel(density, bases, leaf_transfer, parent_transfer, coefficients, partial):
    fan, _, width = bases.shape

    @pl.when(pl.program_id(0) == 0)
    def _():
        partial[...] = jnp.zeros_like(partial)

    values = [
        product(density[:, c * width : (c + 1) * width], bases[c], 1, 1).astype(jnp.bfloat16)
        for c in range(fan)
    ]
    lifted = sum(product(value, leaf_transfer[c]) for c, value in enumerate(values))
    for c in range(0, fan, 2):
        coefficients[c // 2] = jnp.concatenate(values[c : c + 2], axis=1)
    partial[...] += product(lifted.astype(jnp.bfloat16), parent_transfer[0])


def lift(density, bases, leaf_transfer, parent_transfer):
    leaves, rank, width = bases.shape
    sides = density.shape[0]
    parents = parent_transfer.shape[0]
    fan = leaves // parents
    return pl.pallas_call(
        lift_kernel,
        grid=(parents,),
        out_shape=(
            jax.ShapeDtypeStruct((leaves // 2, sides, 2 * rank), jnp.bfloat16),
            jax.ShapeDtypeStruct((sides, rank), jnp.float32),
        ),
        in_specs=[
            pl.BlockSpec((sides, fan * width), lambda p: (0, p)),
            pl.BlockSpec((fan, rank, width), lambda p: (p, 0, 0)),
            pl.BlockSpec((fan, rank, rank), lambda p: (p, 0, 0)),
            pl.BlockSpec((1, rank, rank), lambda p: (p, 0, 0)),
        ],
        out_specs=(
            pl.BlockSpec((fan // 2, sides, 2 * rank), lambda p: (p, 0, 0)),
            pl.BlockSpec((sides, rank), lambda p: (0, 0)),
        ),
        compiler_params=PARAMS,
    )(density, bases, leaf_transfer, parent_transfer)


def split(value):
    high = value.astype(jnp.bfloat16).astype(jnp.float32)
    left = value - high
    middle = left.astype(jnp.bfloat16).astype(jnp.float32)
    return high, middle, left - middle


def near_kernel(
    place, near_list, other_list,
    geo_own, geo_low, geo_high, geo_other, geo_side,
    den_own, den_low, den_high, den_other, den_side,
    near, near_other, task_target, task_source, source, target, density, lhs, column,
    flux_one, flux_two, block_one, block_two, sums,
):
    leaves = geo_own.shape[1]
    width = geo_own.shape[2]
    reach = geo_low.shape[1]
    half = leaves // 2
    region = leaves + reach
    everything = 2 * region
    slots = near_list.shape[0] - 1
    side = place[0]

    def put(ref, row, value):
        for b in range(0, width, LANES):
            ref[b // LANES, pl.ds(row, 8, stride=8), :] = value[:, b : b + LANES]

    def get(ref, row, count):
        return jnp.concatenate(
            [ref[b, pl.ds(row, count), :] for b in range(width // LANES)], axis=1
        )

    def append(lists, base, shift):
        def leaf(i, position):
            t = side * half + i
            live = lists[slots, t]
            for k in range((slots + 1) // 2):
                task_target[(position >> 1) + k] = i + shift
            for k in range(slots):
                task_source[position] = lists[k, t] + base
                position = position + jnp.where(k < live, 1, 0)
            task_source[position] = everything
            return ((position + 1) >> 1) << 1

        return leaf

    for i in range(2):
        task_target[i] = leaves
        task_source[2 * i] = everything
        task_source[2 * i + 1] = everything
    ended = lax.fori_loop(0, half, append(near_list, 0, 0), 4)
    ended = lax.fori_loop(
        0, half, append(other_list, region, half), ended
    )
    pairs = (ended >> 1) - 2
    for i in range(4):
        task_target[pairs + 2 + i] = leaves
        task_source[ended + 2 * i] = everything
        task_source[ended + 2 * i + 1] = everything

    def table(center, base, geo, den):
        for g in range(0, geo.shape[1], 8):
            position = [geo[c, g : g + 8, :width] for c in range(3)]
            normal = [geo[3 + c, g : g + 8, :width] * (1.0 / FOUR_PI) for c in range(3)]
            moved = [value - middle for value, middle in zip(position, center)]
            shift = normal[0] * moved[0] + normal[1] * moved[1] + normal[2] * moved[2]
            row = (base + g) * 8
            for c in range(3):
                put(source, row + c, normal[c])
                put(source, row + 4 + c, position[c])
            put(source, row + 3, shift)
            put(source, row + 7, jnp.zeros_like(shift))
        for l in range(geo.shape[1]):
            density[base + l] = den[:, l * width : (l + 1) * width]

    def aims(center, base, geo):
        def group(i, _):
            place_in = pl.multiple_of(side * half + i * 8, 8)
            row = (base + i * 8) * 8
            one = jnp.ones((8, width), jnp.float32)
            for c in range(3):
                position = geo[c, pl.ds(place_in, 8), :]
                put(target, row + c, position - center[c])
                put(target, row + 4 + c, position)
            put(target, row + 3, -one)
            put(target, row + 7, 0.0 * one)
            return 0

        lax.fori_loop(0, half // 8, group, 0, unroll=True)

    center = [jnp.mean(geo_own[c], keepdims=True) for c in range(3)]
    table(center, 0, geo_own, den_own)

    @pl.when(side == 0)
    def _():
        table(center, leaves, geo_low, den_low)

    @pl.when(side != 0)
    def _():
        table(center, leaves, geo_high, den_high)

    aims(center, 0, geo_own)
    center = [jnp.mean(geo_other[c], keepdims=True) for c in range(3)]
    table(center, region, geo_other, den_other)
    table(center, region + leaves, geo_side, den_side)
    aims(center, half, geo_other)
    density[everything] = jnp.zeros(density.shape[1:], density.dtype)
    for b in range(width // LANES):
        source[b, everything * 8 :, :] = jnp.zeros((8, LANES), jnp.float32)

    rows = lax.broadcasted_iota(jnp.int32, (8, width), 0)
    with_shift = (rows < 4).astype(jnp.float32)
    without = (rows < 3).astype(jnp.float32)

    def prepare(t, _):
        raw = get(target, pl.multiple_of(t * 8, 8), 8)
        high, middle, low = split(raw)
        led = high * with_shift
        second = middle * without
        stacked = jnp.concatenate([led, second, low * without, led, second, led, raw], axis=0)
        turned = stacked.T
        lhs[t] = turned[:, :48].astype(jnp.bfloat16)
        column[t] = turned[:, 48:]
        sums[t] = jnp.zeros(sums.shape[1:], sums.dtype)
        return 0

    lax.fori_loop(0, leaves, prepare, 0, unroll=8)
    sums[leaves] = jnp.zeros(sums.shape[1:], sums.dtype)
    for ref in (flux_one, flux_two, block_one, block_two):
        ref[...] = jnp.zeros_like(ref)

    def weights(s):
        high, middle, low = split(get(source, pl.multiple_of(s * 8, 8), 8))
        return jnp.concatenate([high, high, high, middle, middle, low], axis=0).astype(jnp.bfloat16)

    def multiply(j, block):
        both = jnp.concatenate([density[task_source[2 * j + i]] for i in range(2)], axis=1)
        sums[task_target[j]] += product(both, block[...], 1, 1)

    def evaluate(j, flux, block):
        t = jnp.minimum(task_target[j], leaves - 1)
        pair = [task_source[2 * j + i] for i in range(2)]
        places = [
            jnp.concatenate([get(source, s * 8 + 4 + a, 1) for s in pair], axis=1)
            for a in range(3)
        ]
        for r in range(0, width, CHUNK):
            lines = column[t, r : r + CHUNK, :]
            spread = [
                jnp.broadcast_to(lines[:, 4 + a : 5 + a], (CHUNK, LANES)) for a in range(3)
            ]
            for b in range(0, 2 * width, LANES):
                gap = [spread[a] - places[a][:, b : b + LANES] for a in range(3)]
                squared = gap[0] * gap[0] + gap[1] * gap[1] + (gap[2] * gap[2] + SOFTEN)
                inverse = lax.rsqrt(squared)
                value = flux[r : r + CHUNK, b : b + LANES] * inverse * (inverse * inverse)
                block[r : r + CHUNK, b : b + LANES] = value.astype(jnp.bfloat16)

    def project(j, flux):
        t = jnp.minimum(task_target[j], leaves - 1)
        pair = [task_source[2 * j + i] for i in range(2)]
        flux[...] = product(lhs[t], jnp.concatenate([weights(s) for s in pair], axis=1))

    def step(i, _):
        j = 2 * i
        multiply(j, block_one)
        evaluate(j + 1, flux_two, block_two)
        project(j + 2, flux_one)
        multiply(j + 1, block_two)
        evaluate(j + 2, flux_one, block_one)
        project(j + 3, flux_two)
        return 0

    lax.fori_loop(0, (pairs + 3) >> 1, step, 0)
    for t in range(half):
        near[t] = sums[t]
        near_other[t] = sums[half + t].astype(near_other.dtype)


def near_field(place, lists, geometries, densities):
    leaves, width = geometries[0].shape[1:]
    everything = 2 * (leaves + geometries[1].shape[1])
    sides = densities[0].shape[0]
    slots = lists[0].shape[0] - 1
    most = leaves * (slots // 2 + 1) + 16
    half = (leaves // 2, sides, width)
    return pl.pallas_call(
        near_kernel,
        out_shape=(
            jax.ShapeDtypeStruct(half, jnp.float32),
            jax.ShapeDtypeStruct(half, jnp.bfloat16),
        ),
        in_specs=[SMEM] * 3 + [VMEM] * 10,
        out_specs=(VMEM, VMEM),
        scratch_shapes=[
            pltpu.SMEM((most,), jnp.int32),
            pltpu.SMEM((2 * most,), jnp.int32),
            pltpu.VMEM((width // LANES, (everything + 1) * 8, LANES), jnp.float32),
            pltpu.VMEM((width // LANES, leaves * 8, LANES), jnp.float32),
            pltpu.VMEM((everything + 1, sides, width), jnp.bfloat16),
            pltpu.VMEM((leaves, width, 48), jnp.bfloat16),
            pltpu.VMEM((leaves, width, 8), jnp.float32),
            pltpu.VMEM((width, 2 * width), jnp.float32),
            pltpu.VMEM((width, 2 * width), jnp.float32),
            pltpu.VMEM((width, 2 * width), jnp.bfloat16),
            pltpu.VMEM((width, 2 * width), jnp.bfloat16),
            pltpu.VMEM((leaves + 1, sides, width), jnp.float32),
        ],
        compiler_params=PARAMS,
        cost_estimate=pl.CostEstimate(
            flops=100 * 10**9 // 2, bytes_accessed=8 * 10**6, transcendentals=3 * 10**7
        ),
    )(place, *lists, *geometries, *densities)


def final_kernel(
    place, far_list, top_far, top_proxies, coupled, coef_own, coef_low, coef_high,
    prox_own, prox_low, prox_high, near, near_back, density, bases, leaf_transfer, parent_transfer,
    out, charges, points, lines, parent_local, far,
):
    leaves, rank, width = bases.shape
    group = place[1]
    half = near.shape[0]
    parents = parent_transfer.shape[0]
    fan = leaves // parents
    sides = density.shape[0]
    left = lax.broadcasted_iota(jnp.int32, (sides, LANES), 1) < rank
    row_left = lax.broadcasted_iota(jnp.int32, (1, LANES), 1) < rank

    def duplicate(value):
        return jnp.concatenate([value, value], axis=1)

    top_local = jnp.zeros((sides, rank), jnp.float32)
    stacked = jnp.concatenate(
        [top_proxies[c, pl.ds(group, 1), :] for c in range(3)]
        + [jnp.zeros((5, rank), jnp.float32)], axis=0,
    )
    turned = duplicate(stacked).T[:rank]
    for k in range(top_far.shape[0]):
        node = top_far[k, group]
        squared = jnp.full((rank, rank), SOFTEN, jnp.float32)
        for c in range(3):
            gap = turned[:, c : c + 1] - top_proxies[c, pl.ds(node, 1), :]
            squared = squared + gap * gap
        coupling = (lax.rsqrt(squared) * (1.0 / FOUR_PI)).astype(jnp.bfloat16)
        top_local = top_local + product(coupled[group ^ node], coupling, 1, 1)
    top_local = top_local.astype(jnp.bfloat16)
    for p in range(parents):
        parent_local[p] = product(top_local, parent_transfer[p], 1, 1).astype(jnp.bfloat16)

    for base, ref, prox in (
        (0, coef_low, prox_low), (leaves, coef_own, prox_own), (2 * leaves, coef_high, prox_high)
    ):
        for i in range(leaves // 2):
            value = ref[i].astype(jnp.float32)
            turned = pltpu.roll(value, rank, 1)
            charges[base + 2 * i] = jnp.where(left, value, turned).astype(jnp.bfloat16)
            charges[base + 2 * i + 1] = jnp.where(left, turned, value).astype(jnp.bfloat16)
        for c in range(3):
            if base == leaves:
                points[c, base : base + leaves, :] = duplicate(prox[c])
                continue
            for b in range(2):
                rows = pl.ds(base + b * (leaves // 2), leaves // 2)
                points[c, rows, :] = duplicate(prox[2 * c + b, :, width : width + rank])
    for g in range(0, leaves, 8):
        for c in range(3):
            lines[pl.ds(g * 8 + c, 8, stride=8), :] = points[c, leaves + g : leaves + g + 8, :]
        for c in range(3, 8):
            lines[pl.ds(g * 8 + c, 8, stride=8), :] = jnp.zeros((8, LANES), jnp.float32)

    def far_leaf(t):
        turned = lines[pl.ds(pl.multiple_of(t * 8, 8), 8), :].T[:rank]
        spread = [jnp.broadcast_to(turned[:, c : c + 1], (rank, LANES)) for c in range(3)]
        blocks = []
        values = []
        for q in range(far_list.shape[0] // 2):
            pair = [far_list[2 * q + i, t] for i in range(2)]
            gap = [
                spread[c]
                - jnp.where(
                    row_left, points[c, pl.ds(pair[0], 1), :], points[c, pl.ds(pair[1], 1), :]
                )
                for c in range(3)
            ]
            squared = gap[0] * gap[0] + gap[1] * gap[1] + (gap[2] * gap[2] + SOFTEN)
            blocks.append((lax.rsqrt(squared) * (1.0 / FOUR_PI)).astype(jnp.bfloat16))
            values.append(jnp.where(left, charges[pair[0]], charges[pair[1]]))
        return product(jnp.concatenate(values, axis=1), jnp.concatenate(blocks, axis=1), 1, 1)

    def far_parent(p):
        for i in range(fan):
            far[i] = far_leaf(fan * p + i)

    def down_parent(p):
        start = pl.multiple_of(p * fan, fan)
        transfer = leaf_transfer[pl.ds(start, fan)].reshape(fan * rank, rank)
        whole = product(parent_local[p], transfer, 1, 1)
        for i in range(fan):
            t = fan * p + i
            leaf_local = (far[i] + whole[:, i * rank : (i + 1) * rank]).astype(jnp.bfloat16)
            span = pl.ds(pl.multiple_of(t * width, width), width)
            row = fan * lax.rem(p, half // fan) + i
            mine = p // (half // fan) == place[0]
            nearby = jnp.where(mine, near[row], near_back[row].astype(jnp.float32))
            result = 0.5 * density[:, span].astype(jnp.float32) + nearby
            out[:, span] = result + product(leaf_local, bases[t])

    def both(p, _):
        down_parent(p)
        far_parent(p + 1)
        return 0

    far_parent(0)
    lax.fori_loop(0, parents - 1, both, 0)
    down_parent(parents - 1)


def finish(place, far_list, top_far, top_proxies, coupled, coefs, proxies, near, near_back, density,
           bases, leaf_transfer, parent_transfer):
    leaves, rank, width = bases.shape
    sides = density.shape[0]
    return pl.pallas_call(
        final_kernel,
        out_shape=jax.ShapeDtypeStruct(density.shape, jnp.float32),
        in_specs=[SMEM] * 3 + [VMEM] * 14,
        out_specs=VMEM,
        scratch_shapes=[
            pltpu.VMEM((3 * leaves, sides, LANES), jnp.bfloat16),
            pltpu.VMEM((3, 3 * leaves, LANES), jnp.float32),
            pltpu.VMEM((leaves * 8, LANES), jnp.float32),
            pltpu.VMEM((parent_transfer.shape[0], sides, rank), jnp.bfloat16),
            pltpu.VMEM((leaves // parent_transfer.shape[0], sides, rank), jnp.float32),
        ],
        compiler_params=PARAMS,
    )(place, far_list, top_far, top_proxies, coupled, *coefs, *proxies, near, near_back, density, bases,
      leaf_transfer, parent_transfer)


def per_device(
    density, geometry, near_list, near_count, far_list, bases, proxies, leaf_transfer,
    parent_transfer, top_proxies, top_far,
):
    leaves, _, width = geometry.shape
    devices = lax.axis_size(AXES)
    total = leaves * devices
    group = lax.axis_index("leaf")
    sub = lax.axis_index("sub")
    subs = lax.axis_size("sub")
    groups = lax.axis_size("leaf")
    side = group % 2
    first = (group * subs + sub) * leaves
    place = jnp.stack([side, group]).astype(jnp.int32)

    def swap(value):
        return lax.ppermute(value, "leaf", [(i, i ^ 1) for i in range(groups)])

    reach = leaves // 2
    forward = [(i, (i + 1) % devices) for i in range(devices)]
    backward = [(b, a) for a, b in forward]
    geometry = jnp.transpose(geometry, (1, 0, 2))
    proxies = jnp.transpose(proxies, (1, 0, 2))
    near_list = jnp.transpose(near_list)
    far_list = jnp.transpose(far_list)
    top_proxies = jnp.transpose(top_proxies, (1, 0, 2))
    top_far = jnp.transpose(top_far)

    spread = proxies.reshape(6, leaves // 2, proxies.shape[2])
    geo_low = lax.ppermute(
        jnp.concatenate([geometry[:, leaves - reach :], spread], axis=2), AXES, forward
    )
    geo_high = lax.ppermute(
        jnp.concatenate([geometry[:, :reach], spread], axis=2), AXES, backward
    )
    den_low = lax.ppermute(density[:, (leaves - reach) * width :], AXES, forward)
    den_high = lax.ppermute(density[:, : reach * width], AXES, backward)
    sources = local(near_list, first, total)
    sources = jnp.where(sources < 0, sources + leaves + reach, sources)
    near_list = jnp.concatenate([sources, near_count[None]], axis=0)
    far_list = local(far_list, first, total) + leaves
    other_list = swap(near_list)
    geo_other = swap(geometry)
    den_other = swap(density)

    coefficients, partial = lift(density, bases, leaf_transfer, parent_transfer)

    count = lax.axis_size("sub")
    step = 1
    while step < count:
        partial = partial + lax.ppermute(partial, "sub", [(i, i ^ step) for i in range(count)])
        if step == 1:
            partial, geo_low, geo_high = lax.optimization_barrier((partial, geo_low, geo_high))
        step *= 2
    partial, den_low, den_high = lax.optimization_barrier((partial, den_low, den_high))
    coupled = partial.astype(jnp.bfloat16)[None]
    count = lax.axis_size("leaf")
    step = 1
    while step < count:
        other = lax.ppermute(coupled, "leaf", [(i, i ^ step) for i in range(count)])
        coupled = jnp.concatenate([coupled, other], axis=0)
        step *= 2

    coef_low = lax.ppermute(coefficients, AXES, forward)
    coef_high = lax.ppermute(coefficients, AXES, backward)
    geo_side = swap(jnp.where(side == 0, geo_high, geo_low))
    den_side = swap(jnp.where(side == 0, den_high, den_low))
    coupled, place = lax.optimization_barrier((coupled, place))
    near, near_other = near_field(
        place, (near_list, other_list),
        (geometry, geo_low, geo_high, geo_other, geo_side),
        (density, den_low, den_high, den_other, den_side),
    )
    near_other, coef_low, coef_high = lax.optimization_barrier((near_other, coef_low, coef_high))
    near_back = swap(near_other)
    return finish(
        place, far_list, top_far, top_proxies, coupled,
        (coefficients, coef_low, coef_high), (proxies, geo_low, geo_high),
        near, near_back, density, bases, leaf_transfer, parent_transfer,
    )


def solution(mesh):
    placed = (
        P(None, AXES),
        P(AXES, None, None),
        P(AXES, None),
        P(AXES),
        P(AXES, None),
        P(AXES, None, None),
        P(AXES, None, None),
        P(AXES, None, None),
        P(AXES, None, None),
        P(),
        P(),
    )
    return jax.shard_map(
        per_device, mesh=mesh, in_specs=placed, out_specs=P(None, AXES), check_vma=False
    )
```

```python
import math

import jax
import jax.numpy as jnp
from jax import lax
from jax.experimental import pallas as pl
from jax.experimental.pallas import tpu as pltpu
from jax.sharding import PartitionSpec as P

SOFTEN = 0.01
FOUR_PI = 4.0 * math.pi
AXES = ("leaf", "sub")
LANES = 128
CHUNK = 16
SMEM = pl.BlockSpec(memory_space=pltpu.SMEM)
VMEM = pl.BlockSpec(memory_space=pltpu.VMEM)
PARAMS = pltpu.CompilerParams(vmem_limit_bytes=48 * 1024 * 1024)


def product(left, right, left_dim=1, right_dim=0):
    return lax.dot_general(
        left, right, (((left_dim,), (right_dim,)), ((), ())), preferred_element_type=jnp.float32
    )


def local(leaf, first, total):
    moved = leaf - first + (total + total // 2)
    if total & (total - 1) == 0:
        return (moved & (total - 1)) - total // 2
    return lax.rem(moved, total) - total // 2


def lift_kernel(density, bases, leaf_transfer, parent_transfer, coefficients, partial):
    fan, _, width = bases.shape

    @pl.when(pl.program_id(0) == 0)
    def _():
        partial[...] = jnp.zeros_like(partial)

    values = [
        product(density[:, c * width : (c + 1) * width], bases[c], 1, 1).astype(jnp.bfloat16)
        for c in range(fan)
    ]
    lifted = sum(product(value, leaf_transfer[c]) for c, value in enumerate(values))
    for c in range(0, fan, 2):
        coefficients[c // 2] = jnp.concatenate(values[c : c + 2], axis=1)
    partial[...] += product(lifted.astype(jnp.bfloat16), parent_transfer[0])


def lift(density, bases, leaf_transfer, parent_transfer):
    leaves, rank, width = bases.shape
    sides = density.shape[0]
    parents = parent_transfer.shape[0]
    fan = leaves // parents
    return pl.pallas_call(
        lift_kernel,
        grid=(parents,),
        out_shape=(
            jax.ShapeDtypeStruct((leaves // 2, sides, 2 * rank), jnp.bfloat16),
            jax.ShapeDtypeStruct((sides, rank), jnp.float32),
        ),
        in_specs=[
            pl.BlockSpec((sides, fan * width), lambda p: (0, p)),
            pl.BlockSpec((fan, rank, width), lambda p: (p, 0, 0)),
            pl.BlockSpec((fan, rank, rank), lambda p: (p, 0, 0)),
            pl.BlockSpec((1, rank, rank), lambda p: (p, 0, 0)),
        ],
        out_specs=(
            pl.BlockSpec((fan // 2, sides, 2 * rank), lambda p: (p, 0, 0)),
            pl.BlockSpec((sides, rank), lambda p: (0, 0)),
        ),
        compiler_params=pltpu.CompilerParams(vmem_limit_bytes=60 * 1024 * 1024),
    )(density, bases, leaf_transfer, parent_transfer)


def split(value):
    high = value.astype(jnp.bfloat16).astype(jnp.float32)
    left = value - high
    middle = left.astype(jnp.bfloat16).astype(jnp.float32)
    return high, middle, left - middle


def near_kernel(
    place, near_list, other_list,
    geo_own, geo_low, geo_high, geo_other, geo_side,
    den_own, den_low, den_high, den_other, den_side,
    near, near_other, task_target, task_source, source, target, density, lhs, column,
    flux_one, flux_two, block_one, block_two, sums,
):
    leaves = geo_own.shape[1]
    width = geo_own.shape[2]
    reach = geo_low.shape[1]
    half = leaves // 2
    region = leaves + reach
    everything = 2 * region
    slots = near_list.shape[0] - 1
    side = place[0]

    def put(ref, row, value):
        for b in range(0, width, LANES):
            ref[b // LANES, pl.ds(row, 8, stride=8), :] = value[:, b : b + LANES]

    def get(ref, row, count):
        return jnp.concatenate(
            [ref[b, pl.ds(row, count), :] for b in range(width // LANES)], axis=1
        )

    def append(lists, base, shift):
        def leaf(i, position):
            t = side * half + i
            live = lists[slots, t]
            for k in range((slots + 1) // 2):
                task_target[(position >> 1) + k] = i + shift
            for k in range(slots):
                task_source[position] = lists[k, t] + base
                position = position + jnp.where(k < live, 1, 0)
            task_source[position] = everything
            return ((position + 1) >> 1) << 1

        return leaf

    for i in range(2):
        task_target[i] = leaves
        task_source[2 * i] = everything
        task_source[2 * i + 1] = everything
    ended = lax.fori_loop(0, half, append(near_list, 0, 0), 4)
    ended = lax.fori_loop(
        0, half, append(other_list, region, half), ended
    )
    pairs = (ended >> 1) - 2
    for i in range(4):
        task_target[pairs + 2 + i] = leaves
        task_source[ended + 2 * i] = everything
        task_source[ended + 2 * i + 1] = everything

    def table(center, base, geo, den):
        for g in range(0, geo.shape[1], 8):
            position = [geo[c, g : g + 8, :width] for c in range(3)]
            normal = [geo[3 + c, g : g + 8, :width] * (1.0 / FOUR_PI) for c in range(3)]
            moved = [value - middle for value, middle in zip(position, center)]
            shift = normal[0] * moved[0] + normal[1] * moved[1] + normal[2] * moved[2]
            row = (base + g) * 8
            for c in range(3):
                put(source, row + c, normal[c])
                put(source, row + 4 + c, position[c])
            put(source, row + 3, shift)
            put(source, row + 7, jnp.zeros_like(shift))
        for l in range(geo.shape[1]):
            density[base + l] = den[:, l * width : (l + 1) * width]

    def aims(center, base, geo):
        def group(i, _):
            place_in = pl.multiple_of(side * half + i * 8, 8)
            row = (base + i * 8) * 8
            one = jnp.ones((8, width), jnp.float32)
            for c in range(3):
                position = geo[c, pl.ds(place_in, 8), :]
                put(target, row + c, position - center[c])
                put(target, row + 4 + c, position)
            put(target, row + 3, -one)
            put(target, row + 7, 0.0 * one)
            return 0

        lax.fori_loop(0, half // 8, group, 0, unroll=True)

    center = [jnp.mean(geo_own[c], keepdims=True) for c in range(3)]
    table(center, 0, geo_own, den_own)

    @pl.when(side == 0)
    def _():
        table(center, leaves, geo_low, den_low)

    @pl.when(side != 0)
    def _():
        table(center, leaves, geo_high, den_high)

    aims(center, 0, geo_own)
    center = [jnp.mean(geo_other[c], keepdims=True) for c in range(3)]
    table(center, region, geo_other, den_other)
    table(center, region + leaves, geo_side, den_side)
    aims(center, half, geo_other)
    density[everything] = jnp.zeros(density.shape[1:], density.dtype)
    for b in range(width // LANES):
        source[b, everything * 8 :, :] = jnp.zeros((8, LANES), jnp.float32)

    rows = lax.broadcasted_iota(jnp.int32, (8, width), 0)
    with_shift = (rows < 4).astype(jnp.float32)
    without = (rows < 3).astype(jnp.float32)

    def prepare(t, _):
        raw = get(target, pl.multiple_of(t * 8, 8), 8)
        high, middle, low = split(raw)
        led = high * with_shift
        second = middle * without
        stacked = jnp.concatenate([led, second, low * without, led, second, led, raw], axis=0)
        turned = stacked.T
        lhs[t] = turned[:, :48].astype(jnp.bfloat16)
        column[t] = turned[:, 48:]
        sums[t] = jnp.zeros(sums.shape[1:], sums.dtype)
        return 0

    lax.fori_loop(0, leaves, prepare, 0, unroll=8)
    sums[leaves] = jnp.zeros(sums.shape[1:], sums.dtype)
    for ref in (flux_one, flux_two, block_one, block_two):
        ref[...] = jnp.zeros_like(ref)

    def weights(s):
        high, middle, low = split(get(source, pl.multiple_of(s * 8, 8), 8))
        return jnp.concatenate([high, high, high, middle, middle, low], axis=0).astype(jnp.bfloat16)

    def multiply(j, block):
        both = jnp.concatenate([density[task_source[2 * j + i]] for i in range(2)], axis=1)
        sums[task_target[j]] += product(both, block[...], 1, 1)

    def evaluate(j, flux, block):
        t = jnp.minimum(task_target[j], leaves - 1)
        pair = [task_source[2 * j + i] for i in range(2)]
        places = [
            jnp.concatenate([get(source, s * 8 + 4 + a, 1) for s in pair], axis=1)
            for a in range(3)
        ]
        for r in range(0, width, CHUNK):
            lines = column[t, r : r + CHUNK, :]
            spread = [
                jnp.broadcast_to(lines[:, 4 + a : 5 + a], (CHUNK, LANES)) for a in range(3)
            ]
            for b in range(0, 2 * width, LANES):
                gap = [spread[a] - places[a][:, b : b + LANES] for a in range(3)]
                squared = gap[0] * gap[0] + gap[1] * gap[1] + (gap[2] * gap[2] + SOFTEN)
                inverse = lax.rsqrt(squared)
                value = flux[r : r + CHUNK, b : b + LANES] * inverse * (inverse * inverse)
                block[r : r + CHUNK, b : b + LANES] = value.astype(jnp.bfloat16)

    def project(j, flux):
        t = jnp.minimum(task_target[j], leaves - 1)
        pair = [task_source[2 * j + i] for i in range(2)]
        flux[...] = product(lhs[t], jnp.concatenate([weights(s) for s in pair], axis=1))

    def step(i, _):
        j = 2 * i
        multiply(j, block_one)
        evaluate(j + 1, flux_two, block_two)
        project(j + 2, flux_one)
        multiply(j + 1, block_two)
        evaluate(j + 2, flux_one, block_one)
        project(j + 3, flux_two)
        return 0

    lax.fori_loop(0, (pairs + 3) >> 1, step, 0)
    for t in range(half):
        near[t] = sums[t]
        near_other[t] = sums[half + t].astype(near_other.dtype)


def near_field(place, lists, geometries, densities):
    leaves, width = geometries[0].shape[1:]
    everything = 2 * (leaves + geometries[1].shape[1])
    sides = densities[0].shape[0]
    slots = lists[0].shape[0] - 1
    most = leaves * (slots // 2 + 1) + 16
    half = (leaves // 2, sides, width)
    return pl.pallas_call(
        near_kernel,
        out_shape=(
            jax.ShapeDtypeStruct(half, jnp.float32),
            jax.ShapeDtypeStruct(half, jnp.bfloat16),
        ),
        in_specs=[SMEM] * 3 + [VMEM] * 10,
        out_specs=(VMEM, VMEM),
        scratch_shapes=[
            pltpu.SMEM((most,), jnp.int32),
            pltpu.SMEM((2 * most,), jnp.int32),
            pltpu.VMEM((width // LANES, (everything + 1) * 8, LANES), jnp.float32),
            pltpu.VMEM((width // LANES, leaves * 8, LANES), jnp.float32),
            pltpu.VMEM((everything + 1, sides, width), jnp.bfloat16),
            pltpu.VMEM((leaves, width, 48), jnp.bfloat16),
            pltpu.VMEM((leaves, width, 8), jnp.float32),
            pltpu.VMEM((width, 2 * width), jnp.float32),
            pltpu.VMEM((width, 2 * width), jnp.float32),
            pltpu.VMEM((width, 2 * width), jnp.bfloat16),
            pltpu.VMEM((width, 2 * width), jnp.bfloat16),
            pltpu.VMEM((leaves + 1, sides, width), jnp.float32),
        ],
        compiler_params=PARAMS,
        cost_estimate=pl.CostEstimate(
            flops=100 * 10**9 // 2, bytes_accessed=8 * 10**6, transcendentals=3 * 10**7
        ),
    )(place, *lists, *geometries, *densities)


def final_kernel(
    place, far_list, top_far, top_proxies, coupled, coef_own, coef_low, coef_high,
    prox_own, prox_low, prox_high, near, near_back, density, bases, leaf_transfer, parent_transfer,
    out, charges, points, lines, parent_local, far,
):
    leaves, rank, width = bases.shape
    group = place[1]
    half = near.shape[0]
    parents = parent_transfer.shape[0]
    fan = leaves // parents
    sides = density.shape[0]
    left = lax.broadcasted_iota(jnp.int32, (sides, LANES), 1) < rank
    row_left = lax.broadcasted_iota(jnp.int32, (1, LANES), 1) < rank

    def duplicate(value):
        return jnp.concatenate([value, value], axis=1)

    top_local = jnp.zeros((sides, rank), jnp.float32)
    stacked = jnp.concatenate(
        [top_proxies[c, pl.ds(group, 1), :] for c in range(3)]
        + [jnp.zeros((5, rank), jnp.float32)], axis=0,
    )
    turned = duplicate(stacked).T[:rank]
    for k in range(top_far.shape[0]):
        node = top_far[k, group]
        squared = jnp.full((rank, rank), SOFTEN, jnp.float32)
        for c in range(3):
            gap = turned[:, c : c + 1] - top_proxies[c, pl.ds(node, 1), :]
            squared = squared + gap * gap
        coupling = (lax.rsqrt(squared) * (1.0 / FOUR_PI)).astype(jnp.bfloat16)
        top_local = top_local + product(coupled[group ^ node], coupling, 1, 1)
    top_local = top_local.astype(jnp.bfloat16)
    for p in range(parents):
        parent_local[p] = product(top_local, parent_transfer[p], 1, 1).astype(jnp.bfloat16)

    for base, ref, prox in (
        (0, coef_low, prox_low), (leaves, coef_own, prox_own), (2 * leaves, coef_high, prox_high)
    ):
        for i in range(leaves // 2):
            value = ref[i].astype(jnp.float32)
            turned = pltpu.roll(value, rank, 1)
            charges[base + 2 * i] = jnp.where(left, value, turned).astype(jnp.bfloat16)
            charges[base + 2 * i + 1] = jnp.where(left, turned, value).astype(jnp.bfloat16)
        for c in range(3):
            if base == leaves:
                points[c, base : base + leaves, :] = duplicate(prox[c])
                continue
            for b in range(2):
                rows = pl.ds(base + b * (leaves // 2), leaves // 2)
                points[c, rows, :] = duplicate(prox[2 * c + b, :, width : width + rank])
    for g in range(0, leaves, 8):
        for c in range(3):
            lines[pl.ds(g * 8 + c, 8, stride=8), :] = points[c, leaves + g : leaves + g + 8, :]
        for c in range(3, 8):
            lines[pl.ds(g * 8 + c, 8, stride=8), :] = jnp.zeros((8, LANES), jnp.float32)

    def far_leaf(t):
        turned = lines[pl.ds(pl.multiple_of(t * 8, 8), 8), :].T[:rank]
        spread = [jnp.broadcast_to(turned[:, c : c + 1], (rank, LANES)) for c in range(3)]
        blocks = []
        values = []
        for q in range(far_list.shape[0] // 2):
            pair = [far_list[2 * q + i, t] for i in range(2)]
            gap = [
                spread[c]
                - jnp.where(
                    row_left, points[c, pl.ds(pair[0], 1), :], points[c, pl.ds(pair[1], 1), :]
                )
                for c in range(3)
            ]
            squared = gap[0] * gap[0] + gap[1] * gap[1] + (gap[2] * gap[2] + SOFTEN)
            blocks.append((lax.rsqrt(squared) * (1.0 / FOUR_PI)).astype(jnp.bfloat16))
            values.append(jnp.where(left, charges[pair[0]], charges[pair[1]]))
        return product(jnp.concatenate(values, axis=1), jnp.concatenate(blocks, axis=1), 1, 1)

    def far_parent(p):
        for i in range(fan):
            far[i] = far_leaf(fan * p + i)

    def down_parent(p):
        start = pl.multiple_of(p * fan, fan)
        transfer = leaf_transfer[pl.ds(start, fan)].reshape(fan * rank, rank)
        whole = product(parent_local[p], transfer, 1, 1)
        for i in range(fan):
            t = fan * p + i
            leaf_local = (far[i] + whole[:, i * rank : (i + 1) * rank]).astype(jnp.bfloat16)
            span = pl.ds(pl.multiple_of(t * width, width), width)
            row = fan * lax.rem(p, half // fan) + i
            mine = p // (half // fan) == place[0]
            nearby = jnp.where(mine, near[row], near_back[row].astype(jnp.float32))
            result = 0.5 * density[:, span].astype(jnp.float32) + nearby
            out[:, span] = result + product(leaf_local, bases[t])

    def both(p, _):
        down_parent(p)
        far_parent(p + 1)
        return 0

    far_parent(0)
    lax.fori_loop(0, parents - 1, both, 0)
    down_parent(parents - 1)


def finish(place, far_list, top_far, top_proxies, coupled, coefs, proxies, near, near_back, density,
           bases, leaf_transfer, parent_transfer):
    leaves, rank, width = bases.shape
    sides = density.shape[0]
    return pl.pallas_call(
        final_kernel,
        out_shape=jax.ShapeDtypeStruct(density.shape, jnp.float32),
        in_specs=[SMEM] * 3 + [VMEM] * 14,
        out_specs=VMEM,
        scratch_shapes=[
            pltpu.VMEM((3 * leaves, sides, LANES), jnp.bfloat16),
            pltpu.VMEM((3, 3 * leaves, LANES), jnp.float32),
            pltpu.VMEM((leaves * 8, LANES), jnp.float32),
            pltpu.VMEM((parent_transfer.shape[0], sides, rank), jnp.bfloat16),
            pltpu.VMEM((leaves // parent_transfer.shape[0], sides, rank), jnp.float32),
        ],
        compiler_params=PARAMS,
    )(place, far_list, top_far, top_proxies, coupled, *coefs, *proxies, near, near_back, density, bases,
      leaf_transfer, parent_transfer)


def per_device(
    density, geometry, near_list, near_count, far_list, bases, proxies, leaf_transfer,
    parent_transfer, top_proxies, top_far,
):
    leaves, _, width = geometry.shape
    devices = lax.axis_size(AXES)
    total = leaves * devices
    group = lax.axis_index("leaf")
    sub = lax.axis_index("sub")
    subs = lax.axis_size("sub")
    groups = lax.axis_size("leaf")
    side = group % 2
    first = (group * subs + sub) * leaves
    place = jnp.stack([side, group]).astype(jnp.int32)

    def swap(value):
        return lax.ppermute(value, "leaf", [(i, i ^ 1) for i in range(groups)])

    reach = leaves // 2
    forward = [(i, (i + 1) % devices) for i in range(devices)]
    backward = [(b, a) for a, b in forward]
    geometry = jnp.transpose(geometry, (1, 0, 2))
    proxies = jnp.transpose(proxies, (1, 0, 2))
    near_list = jnp.transpose(near_list)
    far_list = jnp.transpose(far_list)
    top_proxies = jnp.transpose(top_proxies, (1, 0, 2))
    top_far = jnp.transpose(top_far)

    spread = proxies.reshape(6, leaves // 2, proxies.shape[2])
    geo_low = lax.ppermute(
        jnp.concatenate([geometry[:, leaves - reach :], spread], axis=2), AXES, forward
    )
    geo_high = lax.ppermute(
        jnp.concatenate([geometry[:, :reach], spread], axis=2), AXES, backward
    )
    den_low = lax.ppermute(density[:, (leaves - reach) * width :], AXES, forward)
    den_high = lax.ppermute(density[:, : reach * width], AXES, backward)
    sources = local(near_list, first, total)
    sources = jnp.where(sources < 0, sources + leaves + reach, sources)
    near_list = jnp.concatenate([sources, near_count[None]], axis=0)
    far_list = local(far_list, first, total) + leaves
    other_list = swap(near_list)
    geo_other = swap(geometry)
    den_other = swap(density)

    coefficients, partial = lift(density, bases, leaf_transfer, parent_transfer)

    count = lax.axis_size("sub")
    step = 1
    while step < count:
        partial = partial + lax.ppermute(partial, "sub", [(i, i ^ step) for i in range(count)])
        if step == 1:
            partial, geo_low, geo_high, other_list = lax.optimization_barrier(
                (partial, geo_low, geo_high, other_list)
            )
        step *= 2
    partial, den_low, den_high = lax.optimization_barrier((partial, den_low, den_high))
    coupled = partial.astype(jnp.bfloat16)[None]
    count = lax.axis_size("leaf")
    step = 1
    while step < count:
        other = lax.ppermute(coupled, "leaf", [(i, i ^ step) for i in range(count)])
        coupled = jnp.concatenate([coupled, other], axis=0)
        step *= 2

    coef_low = lax.ppermute(coefficients, AXES, forward)
    coef_high = lax.ppermute(coefficients, AXES, backward)
    geo_side = swap(jnp.where(side == 0, geo_high, geo_low))
    den_side = swap(jnp.where(side == 0, den_high, den_low))
    coupled, place = lax.optimization_barrier((coupled, place))
    near, near_other = near_field(
        place, (near_list, other_list),
        (geometry, geo_low, geo_high, geo_other, geo_side),
        (density, den_low, den_high, den_other, den_side),
    )
    near_other, coef_low, coef_high = lax.optimization_barrier((near_other, coef_low, coef_high))
    near_back = swap(near_other)
    return finish(
        place, far_list, top_far, top_proxies, coupled,
        (coefficients, coef_low, coef_high), (proxies, geo_low, geo_high),
        near, near_back, density, bases, leaf_transfer, parent_transfer,
    )


def solution(mesh):
    placed = (
        P(None, AXES),
        P(AXES, None, None),
        P(AXES, None),
        P(AXES),
        P(AXES, None),
        P(AXES, None, None),
        P(AXES, None, None),
        P(AXES, None, None),
        P(AXES, None, None),
        P(),
        P(),
    )
    return jax.shard_map(
        per_device, mesh=mesh, in_specs=placed, out_specs=P(None, AXES), check_vma=False
    )
```

```python
import math

import jax
import jax.numpy as jnp
from jax import lax
from jax.experimental import pallas as pl
from jax.experimental.pallas import tpu as pltpu
from jax.sharding import PartitionSpec as P

SOFTEN = 0.01
FOUR_PI = 4.0 * math.pi
AXES = ("leaf", "sub")
LANES = 128
CHUNK = 16
SMEM = pl.BlockSpec(memory_space=pltpu.SMEM)
VMEM = pl.BlockSpec(memory_space=pltpu.VMEM)
PARAMS = pltpu.CompilerParams(vmem_limit_bytes=48 * 1024 * 1024)


def product(left, right, left_dim=1, right_dim=0):
    return lax.dot_general(
        left, right, (((left_dim,), (right_dim,)), ((), ())), preferred_element_type=jnp.float32
    )


def local(leaf, first, total):
    moved = leaf - first + (total + total // 2)
    if total & (total - 1) == 0:
        return (moved & (total - 1)) - total // 2
    return lax.rem(moved, total) - total // 2


def lift_kernel(density, bases, leaf_transfer, parent_transfer, coefficients, partial):
    fan, _, width = bases.shape

    @pl.when(pl.program_id(0) == 0)
    def _():
        partial[...] = jnp.zeros_like(partial)

    values = [
        product(density[:, c * width : (c + 1) * width], bases[c], 1, 1).astype(jnp.bfloat16)
        for c in range(fan)
    ]
    lifted = sum(product(value, leaf_transfer[c]) for c, value in enumerate(values))
    for c in range(0, fan, 2):
        coefficients[c // 2] = jnp.concatenate(values[c : c + 2], axis=1)
    partial[...] += product(lifted.astype(jnp.bfloat16), parent_transfer[0])


def lift(density, bases, leaf_transfer, parent_transfer):
    leaves, rank, width = bases.shape
    sides = density.shape[0]
    parents = parent_transfer.shape[0]
    fan = leaves // parents
    return pl.pallas_call(
        lift_kernel,
        grid=(parents,),
        out_shape=(
            jax.ShapeDtypeStruct((leaves // 2, sides, 2 * rank), jnp.bfloat16),
            jax.ShapeDtypeStruct((sides, rank), jnp.float32),
        ),
        in_specs=[
            pl.BlockSpec((sides, fan * width), lambda p: (0, p)),
            pl.BlockSpec((fan, rank, width), lambda p: (p, 0, 0)),
            pl.BlockSpec((fan, rank, rank), lambda p: (p, 0, 0)),
            pl.BlockSpec((1, rank, rank), lambda p: (p, 0, 0)),
        ],
        out_specs=(
            pl.BlockSpec((fan // 2, sides, 2 * rank), lambda p: (p, 0, 0)),
            pl.BlockSpec((sides, rank), lambda p: (0, 0)),
        ),
        compiler_params=pltpu.CompilerParams(vmem_limit_bytes=60 * 1024 * 1024),
    )(density, bases, leaf_transfer, parent_transfer)


def split(value):
    high = value.astype(jnp.bfloat16).astype(jnp.float32)
    left = value - high
    middle = left.astype(jnp.bfloat16).astype(jnp.float32)
    return high, middle, left - middle


def near_kernel(
    place, near_list, other_list,
    geo_own, geo_low, geo_high, geo_other, geo_side,
    den_own, den_low, den_high, den_other, den_side,
    near, near_other, task_target, task_source, source, target, density, lhs, column,
    flux_one, flux_two, block_one, block_two, sums,
):
    leaves = geo_own.shape[1]
    width = geo_own.shape[2]
    reach = geo_low.shape[1]
    half = leaves // 2
    region = leaves + reach
    everything = 2 * region
    slots = near_list.shape[0] - 1
    side = place[0]

    def put(ref, row, value):
        for b in range(0, width, LANES):
            ref[b // LANES, pl.ds(row, 8, stride=8), :] = value[:, b : b + LANES]

    def get(ref, row, count):
        return jnp.concatenate(
            [ref[b, pl.ds(row, count), :] for b in range(width // LANES)], axis=1
        )

    def append(lists, base, shift):
        def leaf(i, position):
            t = side * half + i
            live = lists[slots, t]
            for k in range((slots + 1) // 2):
                task_target[(position >> 1) + k] = i + shift
            for k in range(slots):
                task_source[position] = lists[k, t] + base
                position = position + jnp.where(k < live, 1, 0)
            task_source[position] = everything
            return ((position + 1) >> 1) << 1

        return leaf

    for i in range(2):
        task_target[i] = leaves
        task_source[2 * i] = everything
        task_source[2 * i + 1] = everything
    ended = lax.fori_loop(0, half, append(near_list, 0, 0), 4)
    ended = lax.fori_loop(
        0, half, append(other_list, region, half), ended
    )
    pairs = (ended >> 1) - 2
    for i in range(4):
        task_target[pairs + 2 + i] = leaves
        task_source[ended + 2 * i] = everything
        task_source[ended + 2 * i + 1] = everything

    def table(center, base, geo, den):
        for g in range(0, geo.shape[1], 8):
            position = [geo[c, g : g + 8, :width] for c in range(3)]
            normal = [geo[3 + c, g : g + 8, :width] * (1.0 / FOUR_PI) for c in range(3)]
            moved = [value - middle for value, middle in zip(position, center)]
            shift = normal[0] * moved[0] + normal[1] * moved[1] + normal[2] * moved[2]
            row = (base + g) * 8
            for c in range(3):
                put(source, row + c, normal[c])
                put(source, row + 4 + c, position[c])
            put(source, row + 3, shift)
            put(source, row + 7, jnp.zeros_like(shift))
        for l in range(geo.shape[1]):
            density[base + l] = den[:, l * width : (l + 1) * width]

    def aims(center, base, geo):
        def group(i, _):
            place_in = pl.multiple_of(side * half + i * 8, 8)
            row = (base + i * 8) * 8
            one = jnp.ones((8, width), jnp.float32)
            for c in range(3):
                position = geo[c, pl.ds(place_in, 8), :]
                put(target, row + c, position - center[c])
                put(target, row + 4 + c, position)
            put(target, row + 3, -one)
            put(target, row + 7, 0.0 * one)
            return 0

        lax.fori_loop(0, half // 8, group, 0, unroll=True)

    center = [jnp.mean(geo_own[c], keepdims=True) for c in range(3)]
    table(center, 0, geo_own, den_own)

    @pl.when(side == 0)
    def _():
        table(center, leaves, geo_low, den_low)

    @pl.when(side != 0)
    def _():
        table(center, leaves, geo_high, den_high)

    aims(center, 0, geo_own)
    center = [jnp.mean(geo_other[c], keepdims=True) for c in range(3)]
    table(center, region, geo_other, den_other)
    table(center, region + leaves, geo_side, den_side)
    aims(center, half, geo_other)
    density[everything] = jnp.zeros(density.shape[1:], density.dtype)
    for b in range(width // LANES):
        source[b, everything * 8 :, :] = jnp.zeros((8, LANES), jnp.float32)

    rows = lax.broadcasted_iota(jnp.int32, (8, width), 0)
    with_shift = (rows < 4).astype(jnp.float32)
    without = (rows < 3).astype(jnp.float32)

    def prepare(t, _):
        raw = get(target, pl.multiple_of(t * 8, 8), 8)
        high, middle, low = split(raw)
        led = high * with_shift
        second = middle * without
        stacked = jnp.concatenate([led, second, low * without, led, second, led, raw], axis=0)
        turned = stacked.T
        lhs[t] = turned[:, :48].astype(jnp.bfloat16)
        column[t] = turned[:, 48:]
        sums[t] = jnp.zeros(sums.shape[1:], sums.dtype)
        return 0

    lax.fori_loop(0, leaves, prepare, 0, unroll=8)
    sums[leaves] = jnp.zeros(sums.shape[1:], sums.dtype)
    for ref in (flux_one, flux_two, block_one, block_two):
        ref[...] = jnp.zeros_like(ref)

    def weights(s):
        high, middle, low = split(get(source, pl.multiple_of(s * 8, 8), 8))
        return jnp.concatenate([high, high, high, middle, middle, low], axis=0).astype(jnp.bfloat16)

    def multiply(j, block):
        both = jnp.concatenate([density[task_source[2 * j + i]] for i in range(2)], axis=1)
        sums[task_target[j]] += product(both, block[...], 1, 1)

    def evaluate(j, flux, block):
        t = jnp.minimum(task_target[j], leaves - 1)
        pair = [task_source[2 * j + i] for i in range(2)]
        places = [
            jnp.concatenate([get(source, s * 8 + 4 + a, 1) for s in pair], axis=1)
            for a in range(3)
        ]
        for r in range(0, width, CHUNK):
            lines = column[t, r : r + CHUNK, :]
            spread = [
                jnp.broadcast_to(lines[:, 4 + a : 5 + a], (CHUNK, LANES)) for a in range(3)
            ]
            for b in range(0, 2 * width, LANES):
                gap = [spread[a] - places[a][:, b : b + LANES] for a in range(3)]
                squared = gap[0] * gap[0] + gap[1] * gap[1] + (gap[2] * gap[2] + SOFTEN)
                inverse = lax.rsqrt(squared)
                value = flux[r : r + CHUNK, b : b + LANES] * inverse * (inverse * inverse)
                block[r : r + CHUNK, b : b + LANES] = value.astype(jnp.bfloat16)

    def project(j, flux):
        t = jnp.minimum(task_target[j], leaves - 1)
        pair = [task_source[2 * j + i] for i in range(2)]
        flux[...] = product(lhs[t], jnp.concatenate([weights(s) for s in pair], axis=1))

    def step(i, _):
        j = 2 * i
        multiply(j, block_one)
        evaluate(j + 1, flux_two, block_two)
        project(j + 2, flux_one)
        multiply(j + 1, block_two)
        evaluate(j + 2, flux_one, block_one)
        project(j + 3, flux_two)
        return 0

    lax.fori_loop(0, (pairs + 3) >> 1, step, 0)
    for t in range(half):
        near[t] = sums[t]
        near_other[t] = sums[half + t].astype(near_other.dtype)


def near_field(place, lists, geometries, densities):
    leaves, width = geometries[0].shape[1:]
    everything = 2 * (leaves + geometries[1].shape[1])
    sides = densities[0].shape[0]
    slots = lists[0].shape[0] - 1
    most = leaves * (slots // 2 + 1) + 16
    half = (leaves // 2, sides, width)
    return pl.pallas_call(
        near_kernel,
        out_shape=(
            jax.ShapeDtypeStruct(half, jnp.float32),
            jax.ShapeDtypeStruct(half, jnp.bfloat16),
        ),
        in_specs=[SMEM] * 3 + [VMEM] * 10,
        out_specs=(VMEM, VMEM),
        scratch_shapes=[
            pltpu.SMEM((most,), jnp.int32),
            pltpu.SMEM((2 * most,), jnp.int32),
            pltpu.VMEM((width // LANES, (everything + 1) * 8, LANES), jnp.float32),
            pltpu.VMEM((width // LANES, leaves * 8, LANES), jnp.float32),
            pltpu.VMEM((everything + 1, sides, width), jnp.bfloat16),
            pltpu.VMEM((leaves, width, 48), jnp.bfloat16),
            pltpu.VMEM((leaves, width, 8), jnp.float32),
            pltpu.VMEM((width, 2 * width), jnp.float32),
            pltpu.VMEM((width, 2 * width), jnp.float32),
            pltpu.VMEM((width, 2 * width), jnp.bfloat16),
            pltpu.VMEM((width, 2 * width), jnp.bfloat16),
            pltpu.VMEM((leaves + 1, sides, width), jnp.float32),
        ],
        compiler_params=PARAMS,
        cost_estimate=pl.CostEstimate(
            flops=100 * 10**9 // 2, bytes_accessed=8 * 10**6, transcendentals=3 * 10**7
        ),
    )(place, *lists, *geometries, *densities)


def final_kernel(
    place, far_list, top_far, top_proxies, coupled, coef_own, coef_low, coef_high,
    prox_own, prox_low, prox_high, near, near_back, density, bases, leaf_transfer, parent_transfer,
    out, charges, points, lines, parent_local, far,
):
    leaves, rank, width = bases.shape
    group = place[1]
    half = near.shape[0]
    parents = parent_transfer.shape[0]
    fan = leaves // parents
    sides = density.shape[0]
    left = lax.broadcasted_iota(jnp.int32, (sides, LANES), 1) < rank
    row_left = lax.broadcasted_iota(jnp.int32, (1, LANES), 1) < rank

    def duplicate(value):
        return jnp.concatenate([value, value], axis=1)

    top_local = jnp.zeros((sides, rank), jnp.float32)
    stacked = jnp.concatenate(
        [top_proxies[c, pl.ds(group, 1), :] for c in range(3)]
        + [jnp.zeros((5, rank), jnp.float32)], axis=0,
    )
    turned = duplicate(stacked).T[:rank]
    for k in range(top_far.shape[0]):
        node = top_far[k, group]
        squared = jnp.full((rank, rank), SOFTEN, jnp.float32)
        for c in range(3):
            gap = turned[:, c : c + 1] - top_proxies[c, pl.ds(node, 1), :]
            squared = squared + gap * gap
        coupling = (lax.rsqrt(squared) * (1.0 / FOUR_PI)).astype(jnp.bfloat16)
        top_local = top_local + product(coupled[group ^ node], coupling, 1, 1)
    top_local = top_local.astype(jnp.bfloat16)
    for p in range(parents):
        parent_local[p] = product(top_local, parent_transfer[p], 1, 1).astype(jnp.bfloat16)

    for base, ref, prox in (
        (0, coef_low, prox_low), (leaves, coef_own, prox_own), (2 * leaves, coef_high, prox_high)
    ):
        for i in range(leaves // 2):
            value = ref[i].astype(jnp.float32)
            turned = pltpu.roll(value, rank, 1)
            charges[base + 2 * i] = jnp.where(left, value, turned).astype(jnp.bfloat16)
            charges[base + 2 * i + 1] = jnp.where(left, turned, value).astype(jnp.bfloat16)
        for c in range(3):
            if base == leaves:
                points[c, base : base + leaves, :] = duplicate(prox[c])
                continue
            for b in range(2):
                rows = pl.ds(base + b * (leaves // 2), leaves // 2)
                points[c, rows, :] = duplicate(prox[2 * c + b, :, width : width + rank])
    for g in range(0, leaves, 8):
        for c in range(3):
            lines[pl.ds(g * 8 + c, 8, stride=8), :] = points[c, leaves + g : leaves + g + 8, :]
        for c in range(3, 8):
            lines[pl.ds(g * 8 + c, 8, stride=8), :] = jnp.zeros((8, LANES), jnp.float32)

    def far_leaf(t):
        turned = lines[pl.ds(pl.multiple_of(t * 8, 8), 8), :].T[:rank]
        spread = [jnp.broadcast_to(turned[:, c : c + 1], (rank, LANES)) for c in range(3)]
        blocks = []
        values = []
        for q in range(far_list.shape[0] // 2):
            pair = [far_list[2 * q + i, t] for i in range(2)]
            gap = [
                spread[c]
                - jnp.where(
                    row_left, points[c, pl.ds(pair[0], 1), :], points[c, pl.ds(pair[1], 1), :]
                )
                for c in range(3)
            ]
            squared = gap[0] * gap[0] + gap[1] * gap[1] + (gap[2] * gap[2] + SOFTEN)
            blocks.append((lax.rsqrt(squared) * (1.0 / FOUR_PI)).astype(jnp.bfloat16))
            values.append(jnp.where(left, charges[pair[0]], charges[pair[1]]))
        return product(jnp.concatenate(values, axis=1), jnp.concatenate(blocks, axis=1), 1, 1)

    def far_parent(p):
        for i in range(fan):
            far[i] = far_leaf(fan * p + i)

    def down_parent(p):
        start = pl.multiple_of(p * fan, fan)
        transfer = leaf_transfer[pl.ds(start, fan)].reshape(fan * rank, rank)
        whole = product(parent_local[p], transfer, 1, 1)
        for i in range(fan):
            t = fan * p + i
            leaf_local = (far[i] + whole[:, i * rank : (i + 1) * rank]).astype(jnp.bfloat16)
            span = pl.ds(pl.multiple_of(t * width, width), width)
            row = fan * lax.rem(p, half // fan) + i
            mine = p // (half // fan) == place[0]
            nearby = jnp.where(mine, near[row], near_back[row].astype(jnp.float32))
            result = 0.5 * density[:, span].astype(jnp.float32) + nearby
            out[:, span] = result + product(leaf_local, bases[t])

    def both(p, _):
        down_parent(p)
        far_parent(p + 1)
        return 0

    far_parent(0)
    lax.fori_loop(0, parents - 1, both, 0)
    down_parent(parents - 1)


def finish(place, far_list, top_far, top_proxies, coupled, coefs, proxies, near, near_back, density,
           bases, leaf_transfer, parent_transfer):
    leaves, rank, width = bases.shape
    sides = density.shape[0]
    return pl.pallas_call(
        final_kernel,
        out_shape=jax.ShapeDtypeStruct(density.shape, jnp.float32),
        in_specs=[SMEM] * 3 + [VMEM] * 14,
        out_specs=VMEM,
        scratch_shapes=[
            pltpu.VMEM((3 * leaves, sides, LANES), jnp.bfloat16),
            pltpu.VMEM((3, 3 * leaves, LANES), jnp.float32),
            pltpu.VMEM((leaves * 8, LANES), jnp.float32),
            pltpu.VMEM((parent_transfer.shape[0], sides, rank), jnp.bfloat16),
            pltpu.VMEM((leaves // parent_transfer.shape[0], sides, rank), jnp.float32),
        ],
        compiler_params=PARAMS,
    )(place, far_list, top_far, top_proxies, coupled, *coefs, *proxies, near, near_back, density, bases,
      leaf_transfer, parent_transfer)


def per_device(
    density, geometry, near_list, near_count, far_list, bases, proxies, leaf_transfer,
    parent_transfer, top_proxies, top_far,
):
    leaves, _, width = geometry.shape
    devices = lax.axis_size(AXES)
    total = leaves * devices
    group = lax.axis_index("leaf")
    sub = lax.axis_index("sub")
    subs = lax.axis_size("sub")
    groups = lax.axis_size("leaf")
    side = group % 2
    first = (group * subs + sub) * leaves
    place = jnp.stack([side, group]).astype(jnp.int32)

    def swap(value):
        return lax.ppermute(value, "leaf", [(i, i ^ 1) for i in range(groups)])

    reach = leaves // 2
    forward = [(i, (i + 1) % devices) for i in range(devices)]
    backward = [(b, a) for a, b in forward]
    geometry = jnp.transpose(geometry, (1, 0, 2))
    proxies = jnp.transpose(proxies, (1, 0, 2))
    near_list = jnp.transpose(near_list)
    far_list = jnp.transpose(far_list)
    top_proxies = jnp.transpose(top_proxies, (1, 0, 2))
    top_far = jnp.transpose(top_far)

    spread = proxies.reshape(6, leaves // 2, proxies.shape[2])
    geo_low = lax.ppermute(
        jnp.concatenate([geometry[:, leaves - reach :], spread], axis=2), AXES, forward
    )
    geo_high = lax.ppermute(
        jnp.concatenate([geometry[:, :reach], spread], axis=2), AXES, backward
    )
    den_low = lax.ppermute(density[:, (leaves - reach) * width :], AXES, forward)
    den_high = lax.ppermute(density[:, : reach * width], AXES, backward)
    sources = local(near_list, first, total)
    sources = jnp.where(sources < 0, sources + leaves + reach, sources)
    near_list = jnp.concatenate([sources, near_count[None]], axis=0)
    far_list = local(far_list, first, total) + leaves
    other_list = swap(near_list)
    geo_other = swap(geometry)
    den_other = swap(density)

    coefficients, partial = lift(density, bases, leaf_transfer, parent_transfer)

    count = lax.axis_size("sub")
    step = 1
    while step < count:
        partial = partial + lax.ppermute(partial, "sub", [(i, i ^ step) for i in range(count)])
        if step == 1:
            partial, geo_low, geo_high, other_list = lax.optimization_barrier(
                (partial, geo_low, geo_high, other_list)
            )
        step *= 2
    coupled = partial.astype(jnp.bfloat16)[None]
    count = lax.axis_size("leaf")
    step = 1
    while step < count:
        if 2 * step == count:
            coupled, place = lax.optimization_barrier((coupled, place))
        other = lax.ppermute(coupled, "leaf", [(i, i ^ step) for i in range(count)])
        coupled = jnp.concatenate([coupled, other], axis=0)
        if step == 2:
            coupled, den_low, den_high = lax.optimization_barrier((coupled, den_low, den_high))
        step *= 2

    coef_low = lax.ppermute(coefficients, AXES, forward)
    coef_high = lax.ppermute(coefficients, AXES, backward)
    geo_side = swap(jnp.where(side == 0, geo_high, geo_low))
    den_side = swap(jnp.where(side == 0, den_high, den_low))
    near, near_other = near_field(
        place, (near_list, other_list),
        (geometry, geo_low, geo_high, geo_other, geo_side),
        (density, den_low, den_high, den_other, den_side),
    )
    near_other, coef_low, coef_high, coupled = lax.optimization_barrier(
        (near_other, coef_low, coef_high, coupled)
    )
    near_back = swap(near_other)
    return finish(
        place, far_list, top_far, top_proxies, coupled,
        (coefficients, coef_low, coef_high), (proxies, geo_low, geo_high),
        near, near_back, density, bases, leaf_transfer, parent_transfer,
    )


def solution(mesh):
    placed = (
        P(None, AXES),
        P(AXES, None, None),
        P(AXES, None),
        P(AXES),
        P(AXES, None),
        P(AXES, None, None),
        P(AXES, None, None),
        P(AXES, None, None),
        P(AXES, None, None),
        P(),
        P(),
    )
    return jax.shard_map(
        per_device, mesh=mesh, in_specs=placed, out_specs=P(None, AXES), check_vma=False
    )
```

```python
import math

import jax
import jax.numpy as jnp
from jax import lax
from jax.experimental import pallas as pl
from jax.experimental.pallas import tpu as pltpu
from jax.sharding import PartitionSpec as P

SOFTEN = 0.01
FOUR_PI = 4.0 * math.pi
AXES = ("leaf", "sub")
LANES = 128
CHUNK = 16
PARENTS_PER_STEP = 4
SMEM = pl.BlockSpec(memory_space=pltpu.SMEM)
VMEM = pl.BlockSpec(memory_space=pltpu.VMEM)
PARAMS = pltpu.CompilerParams(vmem_limit_bytes=48 * 1024 * 1024)


def product(left, right, left_dim=1, right_dim=0):
    return lax.dot_general(
        left, right, (((left_dim,), (right_dim,)), ((), ())), preferred_element_type=jnp.float32
    )


def local(leaf, first, total):
    moved = leaf - first + (total + total // 2)
    if total & (total - 1) == 0:
        return (moved & (total - 1)) - total // 2
    return lax.rem(moved, total) - total // 2


def lift_kernel(density, bases, leaf_transfer, parent_transfer, coefficients, partial):
    width = bases.shape[2]
    parents = parent_transfer.shape[0]
    fan = bases.shape[0] // parents

    @pl.when(pl.program_id(0) == 0)
    def _():
        partial[...] = jnp.zeros_like(partial)

    values = [
        product(density[:, c * width : (c + 1) * width], bases[c], 1, 1).astype(jnp.bfloat16)
        for c in range(bases.shape[0])
    ]
    for c in range(0, bases.shape[0], 2):
        coefficients[c // 2] = jnp.concatenate(values[c : c + 2], axis=1)
    terms = []
    for p in range(parents):
        lifted = sum(product(values[c], leaf_transfer[c]) for c in range(p * fan, (p + 1) * fan))
        terms.append(product(lifted.astype(jnp.bfloat16), parent_transfer[p]))
    partial[...] += sum(terms)


def lift(density, bases, leaf_transfer, parent_transfer):
    leaves, rank, width = bases.shape
    sides = density.shape[0]
    parents = parent_transfer.shape[0]
    held = PARENTS_PER_STEP
    part = held * (leaves // parents)
    return pl.pallas_call(
        lift_kernel,
        grid=(parents // held,),
        out_shape=(
            jax.ShapeDtypeStruct((leaves // 2, sides, 2 * rank), jnp.bfloat16),
            jax.ShapeDtypeStruct((sides, rank), jnp.float32),
        ),
        in_specs=[
            pl.BlockSpec((sides, part * width), lambda p: (0, p)),
            pl.BlockSpec((part, rank, width), lambda p: (p, 0, 0)),
            pl.BlockSpec((part, rank, rank), lambda p: (p, 0, 0)),
            pl.BlockSpec((held, rank, rank), lambda p: (p, 0, 0)),
        ],
        out_specs=(
            pl.BlockSpec((part // 2, sides, 2 * rank), lambda p: (p, 0, 0)),
            pl.BlockSpec((sides, rank), lambda p: (0, 0)),
        ),
        compiler_params=pltpu.CompilerParams(vmem_limit_bytes=60 * 1024 * 1024),
    )(density, bases, leaf_transfer, parent_transfer)


def split(value):
    high = value.astype(jnp.bfloat16).astype(jnp.float32)
    left = value - high
    middle = left.astype(jnp.bfloat16).astype(jnp.float32)
    return high, middle, left - middle


def near_kernel(
    place, near_list, other_list,
    geo_own, geo_low, geo_high, geo_other, geo_side,
    den_own, den_low, den_high, den_other, den_side,
    near, near_other, task_target, task_source, source, target, density, lhs, column,
    flux_one, flux_two, block_one, block_two, sums,
):
    leaves = geo_own.shape[1]
    width = geo_own.shape[2]
    reach = geo_low.shape[1]
    half = leaves // 2
    region = leaves + reach
    everything = 2 * region
    slots = near_list.shape[0] - 1
    side = place[0]

    def put(ref, row, value):
        for b in range(0, width, LANES):
            ref[b // LANES, pl.ds(row, 8, stride=8), :] = value[:, b : b + LANES]

    def get(ref, row, count):
        return jnp.concatenate(
            [ref[b, pl.ds(row, count), :] for b in range(width // LANES)], axis=1
        )

    def append(lists, base, shift):
        def leaf(i, position):
            t = side * half + i
            live = lists[slots, t]
            for k in range((slots + 1) // 2):
                task_target[(position >> 1) + k] = i + shift
            for k in range(slots):
                task_source[position] = lists[k, t] + base
                position = position + jnp.where(k < live, 1, 0)
            task_source[position] = everything
            return ((position + 1) >> 1) << 1

        return leaf

    for i in range(2):
        task_target[i] = leaves
        task_source[2 * i] = everything
        task_source[2 * i + 1] = everything
    ended = lax.fori_loop(0, half, append(near_list, 0, 0), 4)
    ended = lax.fori_loop(
        0, half, append(other_list, region, half), ended
    )
    pairs = (ended >> 1) - 2
    for i in range(4):
        task_target[pairs + 2 + i] = leaves
        task_source[ended + 2 * i] = everything
        task_source[ended + 2 * i + 1] = everything

    def table(center, base, geo, den):
        for g in range(0, geo.shape[1], 8):
            position = [geo[c, g : g + 8, :width] for c in range(3)]
            normal = [geo[3 + c, g : g + 8, :width] * (1.0 / FOUR_PI) for c in range(3)]
            moved = [value - middle for value, middle in zip(position, center)]
            shift = normal[0] * moved[0] + normal[1] * moved[1] + normal[2] * moved[2]
            row = (base + g) * 8
            for c in range(3):
                put(source, row + c, normal[c])
                put(source, row + 4 + c, position[c])
            put(source, row + 3, shift)
            put(source, row + 7, jnp.zeros_like(shift))
        for l in range(geo.shape[1]):
            density[base + l] = den[:, l * width : (l + 1) * width]

    def aims(center, base, geo):
        def group(i, _):
            place_in = pl.multiple_of(side * half + i * 8, 8)
            row = (base + i * 8) * 8
            one = jnp.ones((8, width), jnp.float32)
            for c in range(3):
                position = geo[c, pl.ds(place_in, 8), :]
                put(target, row + c, position - center[c])
                put(target, row + 4 + c, position)
            put(target, row + 3, -one)
            put(target, row + 7, 0.0 * one)
            return 0

        lax.fori_loop(0, half // 8, group, 0, unroll=True)

    center = [jnp.mean(geo_own[c], keepdims=True) for c in range(3)]
    table(center, 0, geo_own, den_own)

    @pl.when(side == 0)
    def _():
        table(center, leaves, geo_low, den_low)

    @pl.when(side != 0)
    def _():
        table(center, leaves, geo_high, den_high)

    aims(center, 0, geo_own)
    center = [jnp.mean(geo_other[c], keepdims=True) for c in range(3)]
    table(center, region, geo_other, den_other)
    table(center, region + leaves, geo_side, den_side)
    aims(center, half, geo_other)
    density[everything] = jnp.zeros(density.shape[1:], density.dtype)
    for b in range(width // LANES):
        source[b, everything * 8 :, :] = jnp.zeros((8, LANES), jnp.float32)

    rows = lax.broadcasted_iota(jnp.int32, (8, width), 0)
    with_shift = (rows < 4).astype(jnp.float32)
    without = (rows < 3).astype(jnp.float32)

    def prepare(t, _):
        raw = get(target, pl.multiple_of(t * 8, 8), 8)
        high, middle, low = split(raw)
        led = high * with_shift
        second = middle * without
        stacked = jnp.concatenate([led, second, low * without, led, second, led, raw], axis=0)
        turned = stacked.T
        lhs[t] = turned[:, :48].astype(jnp.bfloat16)
        column[t] = turned[:, 48:]
        sums[t] = jnp.zeros(sums.shape[1:], sums.dtype)
        return 0

    lax.fori_loop(0, leaves, prepare, 0, unroll=16)
    sums[leaves] = jnp.zeros(sums.shape[1:], sums.dtype)
    for ref in (flux_one, flux_two, block_one, block_two):
        ref[...] = jnp.zeros_like(ref)

    def weights(s):
        high, middle, low = split(get(source, pl.multiple_of(s * 8, 8), 8))
        return jnp.concatenate([high, high, high, middle, middle, low], axis=0).astype(jnp.bfloat16)

    def multiply(j, block):
        both = jnp.concatenate([density[task_source[2 * j + i]] for i in range(2)], axis=1)
        sums[task_target[j]] += product(both, block[...], 1, 1)

    def evaluate(j, flux, block):
        t = jnp.minimum(task_target[j], leaves - 1)
        pair = [task_source[2 * j + i] for i in range(2)]
        places = [
            jnp.concatenate([get(source, s * 8 + 4 + a, 1) for s in pair], axis=1)
            for a in range(3)
        ]
        for r in range(0, width, CHUNK):
            lines = column[t, r : r + CHUNK, :]
            spread = [
                jnp.broadcast_to(lines[:, 4 + a : 5 + a], (CHUNK, LANES)) for a in range(3)
            ]
            for b in range(0, 2 * width, LANES):
                gap = [spread[a] - places[a][:, b : b + LANES] for a in range(3)]
                squared = gap[0] * gap[0] + gap[1] * gap[1] + (gap[2] * gap[2] + SOFTEN)
                inverse = lax.rsqrt(squared)
                value = flux[r : r + CHUNK, b : b + LANES] * inverse * (inverse * inverse)
                block[r : r + CHUNK, b : b + LANES] = value.astype(jnp.bfloat16)

    def project(j, flux):
        t = jnp.minimum(task_target[j], leaves - 1)
        pair = [task_source[2 * j + i] for i in range(2)]
        flux[...] = product(lhs[t], jnp.concatenate([weights(s) for s in pair], axis=1))

    def step(i, _):
        j = 2 * i
        multiply(j, block_one)
        evaluate(j + 1, flux_two, block_two)
        project(j + 2, flux_one)
        multiply(j + 1, block_two)
        evaluate(j + 2, flux_one, block_one)
        project(j + 3, flux_two)
        return 0

    lax.fori_loop(0, (pairs + 3) >> 1, step, 0)
    for t in range(half):
        near[t] = sums[t]
        near_other[t] = sums[half + t].astype(near_other.dtype)


def near_field(place, lists, geometries, densities):
    leaves, width = geometries[0].shape[1:]
    everything = 2 * (leaves + geometries[1].shape[1])
    sides = densities[0].shape[0]
    slots = lists[0].shape[0] - 1
    most = leaves * (slots // 2 + 1) + 16
    half = (leaves // 2, sides, width)
    return pl.pallas_call(
        near_kernel,
        out_shape=(
            jax.ShapeDtypeStruct(half, jnp.float32),
            jax.ShapeDtypeStruct(half, jnp.bfloat16),
        ),
        in_specs=[SMEM] * 3 + [VMEM] * 10,
        out_specs=(VMEM, VMEM),
        scratch_shapes=[
            pltpu.SMEM((most,), jnp.int32),
            pltpu.SMEM((2 * most,), jnp.int32),
            pltpu.VMEM((width // LANES, (everything + 1) * 8, LANES), jnp.float32),
            pltpu.VMEM((width // LANES, leaves * 8, LANES), jnp.float32),
            pltpu.VMEM((everything + 1, sides, width), jnp.bfloat16),
            pltpu.VMEM((leaves, width, 48), jnp.bfloat16),
            pltpu.VMEM((leaves, width, 8), jnp.float32),
            pltpu.VMEM((width, 2 * width), jnp.float32),
            pltpu.VMEM((width, 2 * width), jnp.float32),
            pltpu.VMEM((width, 2 * width), jnp.bfloat16),
            pltpu.VMEM((width, 2 * width), jnp.bfloat16),
            pltpu.VMEM((leaves + 1, sides, width), jnp.float32),
        ],
        compiler_params=PARAMS,
        cost_estimate=pl.CostEstimate(
            flops=100 * 10**9 // 2, bytes_accessed=8 * 10**6, transcendentals=3 * 10**7
        ),
    )(place, *lists, *geometries, *densities)


def final_kernel(
    place, far_list, top_far, top_proxies, coupled, coef_own, coef_low, coef_high,
    prox_own, prox_low, prox_high, near, near_back, density, bases, leaf_transfer, parent_transfer,
    out, charges, points, lines, parent_local, far,
):
    leaves, rank, width = bases.shape
    group = place[1]
    half = near.shape[0]
    parents = parent_transfer.shape[0]
    fan = leaves // parents
    sides = density.shape[0]
    left = lax.broadcasted_iota(jnp.int32, (sides, LANES), 1) < rank
    row_left = lax.broadcasted_iota(jnp.int32, (1, LANES), 1) < rank

    def duplicate(value):
        return jnp.concatenate([value, value], axis=1)

    top_local = jnp.zeros((sides, rank), jnp.float32)
    stacked = jnp.concatenate(
        [top_proxies[c, pl.ds(group, 1), :] for c in range(3)]
        + [jnp.zeros((5, rank), jnp.float32)], axis=0,
    )
    turned = duplicate(stacked).T[:rank]
    for k in range(top_far.shape[0]):
        node = top_far[k, group]
        squared = jnp.full((rank, rank), SOFTEN, jnp.float32)
        for c in range(3):
            gap = turned[:, c : c + 1] - top_proxies[c, pl.ds(node, 1), :]
            squared = squared + gap * gap
        coupling = (lax.rsqrt(squared) * (1.0 / FOUR_PI)).astype(jnp.bfloat16)
        top_local = top_local + product(coupled[group ^ node], coupling, 1, 1)
    top_local = top_local.astype(jnp.bfloat16)
    for p in range(parents):
        parent_local[p] = product(top_local, parent_transfer[p], 1, 1).astype(jnp.bfloat16)

    for base, ref, prox in (
        (0, coef_low, prox_low), (leaves, coef_own, prox_own), (2 * leaves, coef_high, prox_high)
    ):
        for i in range(leaves // 2):
            value = ref[i].astype(jnp.float32)
            turned = pltpu.roll(value, rank, 1)
            charges[base + 2 * i] = jnp.where(left, value, turned).astype(jnp.bfloat16)
            charges[base + 2 * i + 1] = jnp.where(left, turned, value).astype(jnp.bfloat16)
        for c in range(3):
            if base == leaves:
                points[c, base : base + leaves, :] = duplicate(prox[c])
                continue
            for b in range(2):
                rows = pl.ds(base + b * (leaves // 2), leaves // 2)
                points[c, rows, :] = duplicate(prox[2 * c + b, :, width : width + rank])
    for g in range(0, leaves, 8):
        for c in range(3):
            lines[pl.ds(g * 8 + c, 8, stride=8), :] = points[c, leaves + g : leaves + g + 8, :]
        for c in range(3, 8):
            lines[pl.ds(g * 8 + c, 8, stride=8), :] = jnp.zeros((8, LANES), jnp.float32)

    def far_leaf(t):
        turned = lines[pl.ds(pl.multiple_of(t * 8, 8), 8), :].T[:rank]
        spread = [jnp.broadcast_to(turned[:, c : c + 1], (rank, LANES)) for c in range(3)]
        blocks = []
        values = []
        for q in range(far_list.shape[0] // 2):
            pair = [far_list[2 * q + i, t] for i in range(2)]
            gap = [
                spread[c]
                - jnp.where(
                    row_left, points[c, pl.ds(pair[0], 1), :], points[c, pl.ds(pair[1], 1), :]
                )
                for c in range(3)
            ]
            squared = gap[0] * gap[0] + gap[1] * gap[1] + (gap[2] * gap[2] + SOFTEN)
            blocks.append((lax.rsqrt(squared) * (1.0 / FOUR_PI)).astype(jnp.bfloat16))
            values.append(jnp.where(left, charges[pair[0]], charges[pair[1]]))
        return product(jnp.concatenate(values, axis=1), jnp.concatenate(blocks, axis=1), 1, 1)

    def far_parent(p):
        for i in range(fan):
            far[i] = far_leaf(fan * p + i)

    def down_parent(p):
        start = pl.multiple_of(p * fan, fan)
        transfer = leaf_transfer[pl.ds(start, fan)].reshape(fan * rank, rank)
        whole = product(parent_local[p], transfer, 1, 1)
        for i in range(fan):
            t = fan * p + i
            leaf_local = (far[i] + whole[:, i * rank : (i + 1) * rank]).astype(jnp.bfloat16)
            span = pl.ds(pl.multiple_of(t * width, width), width)
            row = fan * lax.rem(p, half // fan) + i
            mine = p // (half // fan) == place[0]
            nearby = jnp.where(mine, near[row], near_back[row].astype(jnp.float32))
            result = 0.5 * density[:, span].astype(jnp.float32) + nearby
            out[:, span] = result + product(leaf_local, bases[t])

    def both(p, _):
        down_parent(p)
        far_parent(p + 1)
        return 0

    far_parent(0)
    lax.fori_loop(0, parents - 1, both, 0)
    down_parent(parents - 1)


def finish(place, far_list, top_far, top_proxies, coupled, coefs, proxies, near, near_back, density,
           bases, leaf_transfer, parent_transfer):
    leaves, rank, width = bases.shape
    sides = density.shape[0]
    return pl.pallas_call(
        final_kernel,
        out_shape=jax.ShapeDtypeStruct(density.shape, jnp.float32),
        in_specs=[SMEM] * 3 + [VMEM] * 14,
        out_specs=VMEM,
        scratch_shapes=[
            pltpu.VMEM((3 * leaves, sides, LANES), jnp.bfloat16),
            pltpu.VMEM((3, 3 * leaves, LANES), jnp.float32),
            pltpu.VMEM((leaves * 8, LANES), jnp.float32),
            pltpu.VMEM((parent_transfer.shape[0], sides, rank), jnp.bfloat16),
            pltpu.VMEM((leaves // parent_transfer.shape[0], sides, rank), jnp.float32),
        ],
        compiler_params=PARAMS,
    )(place, far_list, top_far, top_proxies, coupled, *coefs, *proxies, near, near_back, density, bases,
      leaf_transfer, parent_transfer)


def per_device(
    density, geometry, near_list, near_count, far_list, bases, proxies, leaf_transfer,
    parent_transfer, top_proxies, top_far,
):
    leaves, _, width = geometry.shape
    devices = lax.axis_size(AXES)
    total = leaves * devices
    group = lax.axis_index("leaf")
    sub = lax.axis_index("sub")
    subs = lax.axis_size("sub")
    groups = lax.axis_size("leaf")
    side = group % 2
    first = (group * subs + sub) * leaves
    place = jnp.stack([side, group]).astype(jnp.int32)

    def swap(value):
        return lax.ppermute(value, "leaf", [(i, i ^ 1) for i in range(groups)])

    reach = leaves // 2
    forward = [(i, (i + 1) % devices) for i in range(devices)]
    backward = [(b, a) for a, b in forward]
    geometry = jnp.transpose(geometry, (1, 0, 2))
    proxies = jnp.transpose(proxies, (1, 0, 2))
    near_list = jnp.transpose(near_list)
    far_list = jnp.transpose(far_list)
    top_proxies = jnp.transpose(top_proxies, (1, 0, 2))
    top_far = jnp.transpose(top_far)

    spread = proxies.reshape(6, leaves // 2, proxies.shape[2])
    geo_low = lax.ppermute(
        jnp.concatenate([geometry[:, leaves - reach :], spread], axis=2), AXES, forward
    )
    geo_high = lax.ppermute(
        jnp.concatenate([geometry[:, :reach], spread], axis=2), AXES, backward
    )
    den_low = lax.ppermute(density[:, (leaves - reach) * width :], AXES, forward)
    den_high = lax.ppermute(density[:, : reach * width], AXES, backward)
    sources = local(near_list, first, total)
    sources = jnp.where(sources < 0, sources + leaves + reach, sources)
    near_list = jnp.concatenate([sources, near_count[None]], axis=0)
    far_list = local(far_list, first, total) + leaves
    other_list = swap(near_list)
    geo_other = swap(geometry)
    den_other = swap(density)

    coefficients, partial = lift(density, bases, leaf_transfer, parent_transfer)

    count = lax.axis_size("sub")
    step = 1
    while step < count:
        partial = partial + lax.ppermute(partial, "sub", [(i, i ^ step) for i in range(count)])
        if step == 1:
            partial, geo_low, geo_high, other_list = lax.optimization_barrier(
                (partial, geo_low, geo_high, other_list)
            )
        step *= 2
    coupled = partial.astype(jnp.bfloat16)[None]
    count = lax.axis_size("leaf")
    step = 1
    while step < count:
        if 2 * step == count:
            coupled, place = lax.optimization_barrier((coupled, place))
        other = lax.ppermute(coupled, "leaf", [(i, i ^ step) for i in range(count)])
        coupled = jnp.concatenate([coupled, other], axis=0)
        if step == 2:
            coupled, den_low, den_high = lax.optimization_barrier((coupled, den_low, den_high))
        step *= 2

    coef_low = lax.ppermute(coefficients, AXES, forward)
    coef_high = lax.ppermute(coefficients, AXES, backward)
    geo_side = swap(jnp.where(side == 0, geo_high, geo_low))
    den_side = swap(jnp.where(side == 0, den_high, den_low))
    near, near_other = near_field(
        place, (near_list, other_list),
        (geometry, geo_low, geo_high, geo_other, geo_side),
        (density, den_low, den_high, den_other, den_side),
    )
    near_other, coef_low, coef_high, coupled = lax.optimization_barrier(
        (near_other, coef_low, coef_high, coupled)
    )
    near_back = swap(near_other)
    return finish(
        place, far_list, top_far, top_proxies, coupled,
        (coefficients, coef_low, coef_high), (proxies, geo_low, geo_high),
        near, near_back, density, bases, leaf_transfer, parent_transfer,
    )


def solution(mesh):
    placed = (
        P(None, AXES),
        P(AXES, None, None),
        P(AXES, None),
        P(AXES),
        P(AXES, None),
        P(AXES, None, None),
        P(AXES, None, None),
        P(AXES, None, None),
        P(AXES, None, None),
        P(),
        P(),
    )
    return jax.shard_map(
        per_device, mesh=mesh, in_specs=placed, out_specs=P(None, AXES), check_vma=False
    )
```

```python
import math

import jax
import jax.numpy as jnp
from jax import lax
from jax.experimental import pallas as pl
from jax.experimental.pallas import tpu as pltpu
from jax.sharding import PartitionSpec as P

SOFTEN = 0.01
FOUR_PI = 4.0 * math.pi
AXES = ("leaf", "sub")
LANES = 128
CHUNK = 16
PARENTS_PER_STEP = 4
SMEM = pl.BlockSpec(memory_space=pltpu.SMEM)
VMEM = pl.BlockSpec(memory_space=pltpu.VMEM)
PARAMS = pltpu.CompilerParams(vmem_limit_bytes=48 * 1024 * 1024)


def product(left, right, left_dim=1, right_dim=0):
    return lax.dot_general(
        left, right, (((left_dim,), (right_dim,)), ((), ())), preferred_element_type=jnp.float32
    )


def local(leaf, first, total):
    moved = leaf - first + (total + total // 2)
    if total & (total - 1) == 0:
        return (moved & (total - 1)) - total // 2
    return lax.rem(moved, total) - total // 2


def lift_kernel(density, bases, leaf_transfer, parent_transfer, coefficients, partial):
    width = bases.shape[2]
    parents = parent_transfer.shape[0]
    fan = bases.shape[0] // parents

    @pl.when(pl.program_id(0) == 0)
    def _():
        partial[...] = jnp.zeros_like(partial)

    values = [
        product(density[:, c * width : (c + 1) * width], bases[c], 1, 1).astype(jnp.bfloat16)
        for c in range(bases.shape[0])
    ]
    for c in range(0, bases.shape[0], 2):
        coefficients[c // 2] = jnp.concatenate(values[c : c + 2], axis=1)
    terms = []
    for p in range(parents):
        lifted = sum(product(values[c], leaf_transfer[c]) for c in range(p * fan, (p + 1) * fan))
        terms.append(product(lifted.astype(jnp.bfloat16), parent_transfer[p]))
    partial[...] += sum(terms)


def lift(density, bases, leaf_transfer, parent_transfer):
    leaves, rank, width = bases.shape
    sides = density.shape[0]
    parents = parent_transfer.shape[0]
    held = PARENTS_PER_STEP
    part = held * (leaves // parents)
    return pl.pallas_call(
        lift_kernel,
        grid=(parents // held,),
        out_shape=(
            jax.ShapeDtypeStruct((leaves // 2, sides, 2 * rank), jnp.bfloat16),
            jax.ShapeDtypeStruct((sides, rank), jnp.float32),
        ),
        in_specs=[
            pl.BlockSpec((sides, part * width), lambda p: (0, p)),
            pl.BlockSpec((part, rank, width), lambda p: (p, 0, 0)),
            pl.BlockSpec((part, rank, rank), lambda p: (p, 0, 0)),
            pl.BlockSpec((held, rank, rank), lambda p: (p, 0, 0)),
        ],
        out_specs=(
            pl.BlockSpec((part // 2, sides, 2 * rank), lambda p: (p, 0, 0)),
            pl.BlockSpec((sides, rank), lambda p: (0, 0)),
        ),
        compiler_params=pltpu.CompilerParams(vmem_limit_bytes=60 * 1024 * 1024),
    )(density, bases, leaf_transfer, parent_transfer)


def split(value):
    high = value.astype(jnp.bfloat16).astype(jnp.float32)
    left = value - high
    middle = left.astype(jnp.bfloat16).astype(jnp.float32)
    return high, middle, left - middle


def near_kernel(
    place, near_list, other_list,
    geo_own, geo_low, geo_high, geo_other, geo_side,
    den_own, den_low, den_high, den_other, den_side,
    near, near_other, task_target, task_source, source, target, density, lhs, column,
    flux_one, flux_two, block_one, block_two, sums,
):
    leaves = geo_own.shape[1]
    width = geo_own.shape[2]
    reach = geo_low.shape[1]
    half = leaves // 2
    region = leaves + reach
    everything = 2 * region
    slots = near_list.shape[0] - 1
    side = place[0]

    def put(ref, row, value):
        for b in range(0, width, LANES):
            ref[b // LANES, pl.ds(row, 8, stride=8), :] = value[:, b : b + LANES]

    def get(ref, row, count):
        return jnp.concatenate(
            [ref[b, pl.ds(row, count), :] for b in range(width // LANES)], axis=1
        )

    def append(lists, base, shift):
        def leaf(i, position):
            t = side * half + i
            live = lists[slots, t]
            for k in range((slots + 1) // 2):
                task_target[(position >> 1) + k] = i + shift
            for k in range(slots):
                task_source[position] = lists[k, t] + base
                position = position + jnp.where(k < live, 1, 0)
            task_source[position] = everything
            return ((position + 1) >> 1) << 1

        return leaf

    for i in range(2):
        task_target[i] = leaves
        task_source[2 * i] = everything
        task_source[2 * i + 1] = everything
    ended = lax.fori_loop(0, half, append(near_list, 0, 0), 4)
    ended = lax.fori_loop(
        0, half, append(other_list, region, half), ended
    )
    pairs = (ended >> 1) - 2
    for i in range(4):
        task_target[pairs + 2 + i] = leaves
        task_source[ended + 2 * i] = everything
        task_source[ended + 2 * i + 1] = everything

    def table(center, base, geo, den):
        for g in range(0, geo.shape[1], 8):
            position = [geo[c, g : g + 8, :width] for c in range(3)]
            normal = [geo[3 + c, g : g + 8, :width] * (1.0 / FOUR_PI) for c in range(3)]
            moved = [value - middle for value, middle in zip(position, center)]
            shift = normal[0] * moved[0] + normal[1] * moved[1] + normal[2] * moved[2]
            row = (base + g) * 8
            for c in range(3):
                put(source, row + c, normal[c])
                put(source, row + 4 + c, position[c])
            put(source, row + 3, shift)
            put(source, row + 7, jnp.zeros_like(shift))
        for l in range(geo.shape[1]):
            density[base + l] = den[:, l * width : (l + 1) * width]

    def aims(center, base, geo):
        def group(i, _):
            place_in = pl.multiple_of(side * half + i * 8, 8)
            row = (base + i * 8) * 8
            one = jnp.ones((8, width), jnp.float32)
            for c in range(3):
                position = geo[c, pl.ds(place_in, 8), :]
                put(target, row + c, position - center[c])
                put(target, row + 4 + c, position)
            put(target, row + 3, -one)
            put(target, row + 7, 0.0 * one)
            return 0

        lax.fori_loop(0, half // 8, group, 0, unroll=True)

    center = [jnp.mean(geo_own[c], keepdims=True) for c in range(3)]
    table(center, 0, geo_own, den_own)

    @pl.when(side == 0)
    def _():
        table(center, leaves, geo_low, den_low)

    @pl.when(side != 0)
    def _():
        table(center, leaves, geo_high, den_high)

    aims(center, 0, geo_own)
    center = [jnp.mean(geo_other[c], keepdims=True) for c in range(3)]
    table(center, region, geo_other, den_other)
    table(center, region + leaves, geo_side, den_side)
    aims(center, half, geo_other)
    density[everything] = jnp.zeros(density.shape[1:], density.dtype)
    for b in range(width // LANES):
        source[b, everything * 8 :, :] = jnp.zeros((8, LANES), jnp.float32)

    rows = lax.broadcasted_iota(jnp.int32, (8, width), 0)
    with_shift = (rows < 4).astype(jnp.float32)
    without = (rows < 3).astype(jnp.float32)

    def prepare(t, _):
        raw = get(target, pl.multiple_of(t * 8, 8), 8)
        high, middle, low = split(raw)
        led = high * with_shift
        second = middle * without
        stacked = jnp.concatenate([led, second, low * without, led, second, led, raw], axis=0)
        turned = stacked.T
        lhs[t] = turned[:, :48].astype(jnp.bfloat16)
        column[t] = turned[:, 48:]
        sums[t] = jnp.zeros(sums.shape[1:], sums.dtype)
        return 0

    lax.fori_loop(0, leaves, prepare, 0, unroll=16)
    sums[leaves] = jnp.zeros(sums.shape[1:], sums.dtype)
    for ref in (flux_one, flux_two, block_one, block_two):
        ref[...] = jnp.zeros_like(ref)

    def weights(s):
        high, middle, low = split(get(source, pl.multiple_of(s * 8, 8), 8))
        return jnp.concatenate([high, high, high, middle, middle, low], axis=0).astype(jnp.bfloat16)

    def multiply(j, block):
        both = jnp.concatenate([density[task_source[2 * j + i]] for i in range(2)], axis=1)
        sums[task_target[j]] += product(both, block[...], 1, 1)

    def evaluate(j, flux, block):
        t = jnp.minimum(task_target[j], leaves - 1)
        pair = [task_source[2 * j + i] for i in range(2)]
        places = [
            jnp.concatenate([get(source, s * 8 + 4 + a, 1) for s in pair], axis=1)
            for a in range(3)
        ]
        for r in range(0, width, CHUNK):
            lines = column[t, r : r + CHUNK, :]
            spread = [
                jnp.broadcast_to(lines[:, 4 + a : 5 + a], (CHUNK, LANES)) for a in range(3)
            ]
            for b in range(0, 2 * width, LANES):
                gap = [spread[a] - places[a][:, b : b + LANES] for a in range(3)]
                squared = gap[0] * gap[0] + gap[1] * gap[1] + (gap[2] * gap[2] + SOFTEN)
                inverse = lax.rsqrt(squared)
                value = flux[r : r + CHUNK, b : b + LANES] * inverse * (inverse * inverse)
                block[r : r + CHUNK, b : b + LANES] = value.astype(jnp.bfloat16)

    def project(j, flux):
        t = jnp.minimum(task_target[j], leaves - 1)
        pair = [task_source[2 * j + i] for i in range(2)]
        flux[...] = product(lhs[t], jnp.concatenate([weights(s) for s in pair], axis=1))

    def step(i, _):
        j = 2 * i
        multiply(j, block_one)
        evaluate(j + 1, flux_two, block_two)
        project(j + 2, flux_one)
        multiply(j + 1, block_two)
        evaluate(j + 2, flux_one, block_one)
        project(j + 3, flux_two)
        return 0

    lax.fori_loop(0, (pairs + 3) >> 1, step, 0)
    for t in range(half):
        near[t] = sums[t]
        near_other[t] = sums[half + t].astype(near_other.dtype)


def near_field(place, lists, geometries, densities):
    leaves, width = geometries[0].shape[1:]
    everything = 2 * (leaves + geometries[1].shape[1])
    sides = densities[0].shape[0]
    slots = lists[0].shape[0] - 1
    most = leaves * (slots // 2 + 1) + 16
    half = (leaves // 2, sides, width)
    return pl.pallas_call(
        near_kernel,
        out_shape=(
            jax.ShapeDtypeStruct(half, jnp.float32),
            jax.ShapeDtypeStruct(half, jnp.bfloat16),
        ),
        in_specs=[SMEM] * 3 + [VMEM] * 10,
        out_specs=(VMEM, VMEM),
        scratch_shapes=[
            pltpu.SMEM((most,), jnp.int32),
            pltpu.SMEM((2 * most,), jnp.int32),
            pltpu.VMEM((width // LANES, (everything + 1) * 8, LANES), jnp.float32),
            pltpu.VMEM((width // LANES, leaves * 8, LANES), jnp.float32),
            pltpu.VMEM((everything + 1, sides, width), jnp.bfloat16),
            pltpu.VMEM((leaves, width, 48), jnp.bfloat16),
            pltpu.VMEM((leaves, width, 8), jnp.float32),
            pltpu.VMEM((width, 2 * width), jnp.float32),
            pltpu.VMEM((width, 2 * width), jnp.float32),
            pltpu.VMEM((width, 2 * width), jnp.bfloat16),
            pltpu.VMEM((width, 2 * width), jnp.bfloat16),
            pltpu.VMEM((leaves + 1, sides, width), jnp.float32),
        ],
        compiler_params=PARAMS,
        cost_estimate=pl.CostEstimate(
            flops=100 * 10**9 // 2, bytes_accessed=8 * 10**6, transcendentals=3 * 10**7
        ),
    )(place, *lists, *geometries, *densities)


def final_kernel(
    place, far_list, top_far, top_proxies, coupled, coef_own, coef_low, coef_high,
    prox_own, prox_low, prox_high, near, near_back, density, bases, leaf_transfer, parent_transfer,
    out, charges, points, lines, parent_local, far,
):
    leaves, rank, width = bases.shape
    group = place[1]
    half = near.shape[0]
    parents = parent_transfer.shape[0]
    fan = leaves // parents
    sides = density.shape[0]
    left = lax.broadcasted_iota(jnp.int32, (sides, LANES), 1) < rank
    row_left = lax.broadcasted_iota(jnp.int32, (1, LANES), 1) < rank

    def duplicate(value):
        return jnp.concatenate([value, value], axis=1)

    top_local = jnp.zeros((sides, rank), jnp.float32)
    stacked = jnp.concatenate(
        [top_proxies[c, pl.ds(group, 1), :] for c in range(3)]
        + [jnp.zeros((5, rank), jnp.float32)], axis=0,
    )
    turned = duplicate(stacked).T[:rank]
    for k in range(top_far.shape[0]):
        node = top_far[k, group]
        squared = jnp.full((rank, rank), SOFTEN, jnp.float32)
        for c in range(3):
            gap = turned[:, c : c + 1] - top_proxies[c, pl.ds(node, 1), :]
            squared = squared + gap * gap
        coupling = (lax.rsqrt(squared) * (1.0 / FOUR_PI)).astype(jnp.bfloat16)
        top_local = top_local + product(coupled[group ^ node], coupling, 1, 1)
    top_local = top_local.astype(jnp.bfloat16)
    for p in range(parents):
        parent_local[p] = product(top_local, parent_transfer[p], 1, 1).astype(jnp.bfloat16)

    for base, ref, prox in (
        (0, coef_low, prox_low), (leaves, coef_own, prox_own), (2 * leaves, coef_high, prox_high)
    ):
        for i in range(leaves // 2):
            value = ref[i].astype(jnp.float32)
            turned = pltpu.roll(value, rank, 1)
            charges[base + 2 * i] = jnp.where(left, value, turned).astype(jnp.bfloat16)
            charges[base + 2 * i + 1] = jnp.where(left, turned, value).astype(jnp.bfloat16)
        for c in range(3):
            if base == leaves:
                points[c, base : base + leaves, :] = duplicate(prox[c])
                continue
            for b in range(2):
                rows = pl.ds(base + b * (leaves // 2), leaves // 2)
                points[c, rows, :] = duplicate(prox[2 * c + b, :, width : width + rank])
    for g in range(0, leaves, 8):
        for c in range(3):
            lines[pl.ds(g * 8 + c, 8, stride=8), :] = points[c, leaves + g : leaves + g + 8, :]
        for c in range(3, 8):
            lines[pl.ds(g * 8 + c, 8, stride=8), :] = jnp.zeros((8, LANES), jnp.float32)

    def far_leaf(t):
        turned = lines[pl.ds(pl.multiple_of(t * 8, 8), 8), :].T[:rank]
        spread = [jnp.broadcast_to(turned[:, c : c + 1], (rank, LANES)) for c in range(3)]
        blocks = []
        values = []
        for q in range(far_list.shape[0] // 2):
            pair = [far_list[2 * q + i, t] for i in range(2)]
            gap = [
                spread[c]
                - jnp.where(
                    row_left, points[c, pl.ds(pair[0], 1), :], points[c, pl.ds(pair[1], 1), :]
                )
                for c in range(3)
            ]
            squared = gap[0] * gap[0] + gap[1] * gap[1] + (gap[2] * gap[2] + SOFTEN)
            blocks.append((lax.rsqrt(squared) * (1.0 / FOUR_PI)).astype(jnp.bfloat16))
            values.append(jnp.where(left, charges[pair[0]], charges[pair[1]]))
        return product(jnp.concatenate(values, axis=1), jnp.concatenate(blocks, axis=1), 1, 1)

    def far_parent(p):
        for i in range(fan):
            far[i] = far_leaf(fan * p + i)

    def down_parent(p):
        start = pl.multiple_of(p * fan, fan)
        transfer = leaf_transfer[pl.ds(start, fan)].reshape(fan * rank, rank)
        whole = product(parent_local[p], transfer, 1, 1)
        for i in range(fan):
            t = fan * p + i
            leaf_local = (far[i] + whole[:, i * rank : (i + 1) * rank]).astype(jnp.bfloat16)
            span = pl.ds(pl.multiple_of(t * width, width), width)
            row = fan * lax.rem(p, half // fan) + i
            mine = p // (half // fan) == place[0]
            nearby = jnp.where(mine, near[row], near_back[row].astype(jnp.float32))
            result = 0.5 * density[:, span].astype(jnp.float32) + nearby
            out[:, span] = result + product(leaf_local, bases[t])

    def both(p, _):
        down_parent(p)
        far_parent(p + 1)
        return 0

    far_parent(0)
    lax.fori_loop(0, parents - 1, both, 0)
    down_parent(parents - 1)


def finish(place, far_list, top_far, top_proxies, coupled, coefs, proxies, near, near_back, density,
           bases, leaf_transfer, parent_transfer):
    leaves, rank, width = bases.shape
    sides = density.shape[0]
    return pl.pallas_call(
        final_kernel,
        out_shape=jax.ShapeDtypeStruct(density.shape, jnp.float32),
        in_specs=[SMEM] * 3 + [VMEM] * 14,
        out_specs=VMEM,
        scratch_shapes=[
            pltpu.VMEM((3 * leaves, sides, LANES), jnp.bfloat16),
            pltpu.VMEM((3, 3 * leaves, LANES), jnp.float32),
            pltpu.VMEM((leaves * 8, LANES), jnp.float32),
            pltpu.VMEM((parent_transfer.shape[0], sides, rank), jnp.bfloat16),
            pltpu.VMEM((leaves // parent_transfer.shape[0], sides, rank), jnp.float32),
        ],
        compiler_params=PARAMS,
    )(place, far_list, top_far, top_proxies, coupled, *coefs, *proxies, near, near_back, density, bases,
      leaf_transfer, parent_transfer)


def per_device(
    density, geometry, near_list, near_count, far_list, bases, proxies, leaf_transfer,
    parent_transfer, top_proxies, top_far,
):
    leaves, _, width = geometry.shape
    devices = lax.axis_size(AXES)
    total = leaves * devices
    group = lax.axis_index("leaf")
    sub = lax.axis_index("sub")
    subs = lax.axis_size("sub")
    groups = lax.axis_size("leaf")
    side = group % 2
    first = (group * subs + sub) * leaves
    place = jnp.stack([side, group]).astype(jnp.int32)

    def swap(value):
        return lax.ppermute(value, "leaf", [(i, i ^ 1) for i in range(groups)])

    reach = leaves // 2
    forward = [(i, (i + 1) % devices) for i in range(devices)]
    backward = [(b, a) for a, b in forward]
    geometry = jnp.transpose(geometry, (1, 0, 2))
    proxies = jnp.transpose(proxies, (1, 0, 2))
    near_list = jnp.transpose(near_list)
    far_list = jnp.transpose(far_list)
    top_proxies = jnp.transpose(top_proxies, (1, 0, 2))
    top_far = jnp.transpose(top_far)

    spread = proxies.reshape(6, leaves // 2, proxies.shape[2])
    geo_low = lax.ppermute(
        jnp.concatenate([geometry[:, leaves - reach :], spread], axis=2), AXES, forward
    )
    geo_high = lax.ppermute(
        jnp.concatenate([geometry[:, :reach], spread], axis=2), AXES, backward
    )
    den_low = lax.ppermute(density[:, (leaves - reach) * width :], AXES, forward)
    den_high = lax.ppermute(density[:, : reach * width], AXES, backward)
    sources = local(near_list, first, total)
    sources = jnp.where(sources < 0, sources + leaves + reach, sources)
    near_list = jnp.concatenate([sources, near_count[None]], axis=0)
    far_list = local(far_list, first, total) + leaves
    other_list = swap(near_list)
    geo_other = swap(geometry)
    den_other = swap(density)

    coefficients, partial = lift(density, bases, leaf_transfer, parent_transfer)

    count = lax.axis_size("sub")
    step = 1
    while step < count:
        partial = partial + lax.ppermute(partial, "sub", [(i, i ^ step) for i in range(count)])
        if step == 1:
            partial, geo_low, geo_high = lax.optimization_barrier((partial, geo_low, geo_high))
        if step == 2:
            partial, den_low, den_high, other_list = lax.optimization_barrier(
                (partial, den_low, den_high, other_list)
            )
        step *= 2
    coupled = partial.astype(jnp.bfloat16)[None]
    count = lax.axis_size("leaf")
    step = 1
    while step < count:
        if 2 * step == count:
            coupled, place = lax.optimization_barrier((coupled, place))
        other = lax.ppermute(coupled, "leaf", [(i, i ^ step) for i in range(count)])
        coupled = jnp.concatenate([coupled, other], axis=0)
        step *= 2

    coef_low = lax.ppermute(coefficients, AXES, forward)
    coef_high = lax.ppermute(coefficients, AXES, backward)
    geo_side = swap(jnp.where(side == 0, geo_high, geo_low))
    den_side = swap(jnp.where(side == 0, den_high, den_low))
    near, near_other = near_field(
        place, (near_list, other_list),
        (geometry, geo_low, geo_high, geo_other, geo_side),
        (density, den_low, den_high, den_other, den_side),
    )
    near_other, coef_low, coef_high, coupled = lax.optimization_barrier(
        (near_other, coef_low, coef_high, coupled)
    )
    near_back = swap(near_other)
    return finish(
        place, far_list, top_far, top_proxies, coupled,
        (coefficients, coef_low, coef_high), (proxies, geo_low, geo_high),
        near, near_back, density, bases, leaf_transfer, parent_transfer,
    )


def solution(mesh):
    placed = (
        P(None, AXES),
        P(AXES, None, None),
        P(AXES, None),
        P(AXES),
        P(AXES, None),
        P(AXES, None, None),
        P(AXES, None, None),
        P(AXES, None, None),
        P(AXES, None, None),
        P(),
        P(),
    )
    return jax.shard_map(
        per_device, mesh=mesh, in_specs=placed, out_specs=P(None, AXES), check_vma=False
    )
```
